512 devices in a mesh: grp: 16 (over x, y), pb: 4 (over z_hi), ka: 8 (over z_lo, core).
Axes of the slice: x: 4, y: 4, z: 16 (z_hi: 4, z_lo: 4; z = z_hi * 4 + z_lo), core: 2. Of those that a mesh axis runs over, the one named last changes fastest.
Arguments:
- lengths: int32 [16], P('grp'), may hold values from 64 to 256, as said below
- single: bfloat16 [16, 8, 256, 768], P('grp', None, ('pb', 'ka')), may hold values from -6 to 6
- attn_gain: float32 [768], replicated, may hold values from 0.25 to 1.75
- w_query: bfloat16 [768, 768], P(('grp', 'pb')), may hold values from -0.21875 to 0.21875
- w_key: bfloat16 [768, 768], P(('grp', 'pb')), may hold values from -0.21875 to 0.21875
- w_value: bfloat16 [768, 768], P(('grp', 'pb')), may hold values from -0.21875 to 0.21875
- w_gate: bfloat16 [768, 768], P(('grp', 'pb')), may hold values from -0.21875 to 0.21875
- w_out: bfloat16 [768, 768], P(('grp', 'pb'), 'ka'), may hold values from -0.21875 to 0.21875
- pair_rep: bfloat16 [16, 256, 4, 64, 128], P('grp', 'pb', None, 'ka'), may hold values from -16 to 16
- pair_gain: float32 [128], replicated, may hold values from 0.25 to 1.75
- pair_proj: float32 [128, 16], replicated, may hold values from -3 to 3
- trans_gain: float32 [768], replicated, may hold values from 0.25 to 1.75
- w_swish: bfloat16 [768, 1536], P(('grp', 'pb'), 'ka'), may hold values from -0.21875 to 0.21875
- w_up: bfloat16 [768, 1536], P(('grp', 'pb'), 'ka'), may hold values from -0.21875 to 0.21875
- w_down: bfloat16 [1536, 768], P('ka', ('grp', 'pb')), may hold values from -0.15625 to 0.15625
Outputs:
- updated: bfloat16 [16, 8, 256, 768], P('grp', None, ('pb', 'ka'))
The draws below stay inside these ranges and needn't reach their ends.
Inputs may be any that keep to these rules, and one draw needn't show every extreme that they name: `lengths`: tokens of a complex; positions from it on are padding; some complex has exactly 256 tokens.
All inputs are finite; a program needn't handle non-finite values.
Results may differ from the reference program's by a relative error of at most 0.014.
Values may be sent and summed in bfloat16 or wider, within the bound.
No kernel may reach another device: no remote copies, remote signals or barrier semaphores. Data moves between devices by JAX's collectives and lax.ppermute only.
A program may use at most 192 MiB of HBM per device.

```python
import math
import jax
import jax.numpy as jnp
from jax import lax

D = 768
HEADS = 16
CP = 128
FF = 1536
SAMPLES = 8
GROUPS = 16
L = 256
KB = 64
N_PB = 4


def draw_lengths(key, part):
    key = jax.random.fold_in(key, 5)
    first_key = jax.random.fold_in(key, 1)
    second_key = jax.random.fold_in(key, 2)
    drawn = jax.random.randint(first_key, (GROUPS,), L // 4, L + 1)
    longest = jax.random.randint(second_key, (), 0, GROUPS)
    return jnp.where(jnp.arange(GROUPS, dtype=jnp.int32) == longest, L, drawn).astype(jnp.int32)


def draw_pair_rep(key, part):
    key = jax.random.fold_in(key, 11)
    shape = (GROUPS, L, N_PB, KB, CP)
    return jax.random.truncated_normal(key, -6.0, 6.0, shape).astype(jnp.bfloat16)


def draw_pair_proj(key, part):
    key = jax.random.fold_in(key, 23)
    base = jax.random.truncated_normal(jax.random.fold_in(key, 1), -6.0, 6.0, (CP, HEADS)) / math.sqrt(CP)
    return base


def block_levels(rng, shape, pieces, low, top_value):
    gain = 1.0
    for axis_at, parts in pieces:
        heights = jax.random.uniform(jax.random.fold_in(jax.random.fold_in(rng, 6), axis_at), (parts,), jnp.float32, low / len(pieces), top_value / len(pieces))
        gain = gain * jnp.repeat(jnp.exp(heights), shape[axis_at] // parts).reshape((-1,) + (1,) * (len(shape) - 1 - axis_at))
    return gain


def gaussian(key, extent, deviation, most, shards=(), held_as=jnp.bfloat16):
    factor_of = block_levels(key, extent, shards, -0.22, 0.18) if shards else 1.0
    values = jax.random.normal(key, extent, jnp.float32) * deviation * factor_of
    return jnp.minimum(jnp.maximum(values, -most), most).astype(held_as)


def setup_inputs(seed: int = 0) -> dict:
    key_of = jax.random.split(jax.random.key(seed), 16)
    return {
        "lengths": draw_lengths(jax.random.fold_in(key_of[15], 71), 0),
        "single": gaussian(key_of[1], (GROUPS, SAMPLES, L, D), 1.0, 6.0, ((0, 16), (2, 32))),
        "attn_gain": jnp.clip(1.0 + 0.15 * jax.random.normal(key_of[2], (D,), jnp.float32), 0.25, 1.75),
        "w_query": gaussian(key_of[3], (D, D), D ** -0.5, 0.21875, ((0, 64),)),
        "w_key": gaussian(key_of[4], (D, D), D ** -0.5, 0.21875, ((0, 64),)),
        "w_value": gaussian(key_of[5], (D, D), D ** -0.5, 0.21875, ((0, 64),)),
        "w_gate": gaussian(key_of[6], (D, D), D ** -0.5, 0.21875, ((0, 64),)),
        "w_out": gaussian(key_of[7], (D, D), D ** -0.5, 0.21875, ((0, 64), (1, 8))),
        "pair_rep": draw_pair_rep(jax.random.fold_in(key_of[15], 71), 0),
        "pair_gain": jnp.clip(1.0 + 0.15 * jax.random.normal(key_of[9], (CP,), jnp.float32), 0.25, 1.75),
        "pair_proj": draw_pair_proj(jax.random.fold_in(key_of[15], 71), 0),
        "trans_gain": jnp.clip(1.0 + 0.15 * jax.random.normal(key_of[11], (D,), jnp.float32), 0.25, 1.75),
        "w_swish": gaussian(key_of[12], (D, FF), D ** -0.5, 0.21875, ((0, 64), (1, 8))),
        "w_up": gaussian(key_of[13], (D, FF), D ** -0.5, 0.21875, ((0, 64), (1, 8))),
        "w_down": gaussian(key_of[14], (FF, D), FF ** -0.5, 0.15625, ((0, 8), (1, 64))),
    }


epsilon = 1e-05
very_negative = -1e+30

def layer_norm(inputs, scale_gain):
    mean_val = lax.optimization_barrier(jnp.mean(inputs, axis=-1, keepdims=True))
    centred = inputs - mean_val
    spread = lax.optimization_barrier(jnp.mean(centred * centred, axis=-1, keepdims=True))
    return centred * lax.rsqrt(spread + epsilon) * scale_gain

def project(inputs, weight):
    return jnp.dot(inputs, weight, preferred_element_type=jnp.float32)

def reference(lengths, single, attn_gain, w_query, w_key, w_value, w_gate, w_out, pair_rep, pair_gain, pair_proj, trans_gain, w_swish, w_up, w_down):
    head_dim = D // HEADS

    def one_group(packed):
        length, group_single, group_pair = packed
        normed = layer_norm(group_single.astype(jnp.float32), attn_gain).astype(jnp.bfloat16).reshape(SAMPLES * L, D)
        queries = project(normed, w_query).astype(jnp.bfloat16).reshape(SAMPLES, L, HEADS, head_dim)
        key_proj = project(normed, w_key).astype(jnp.bfloat16).reshape(SAMPLES, L, HEADS, head_dim)
        value_proj = project(normed, w_value).astype(jnp.bfloat16).reshape(SAMPLES, L, HEADS, head_dim)
        gate_vals = jax.nn.sigmoid(project(normed, w_gate)).astype(jnp.bfloat16).reshape(SAMPLES, L, D)
        key_live = jnp.arange(L, dtype=jnp.int32) < length
        pair_full = group_pair.reshape(L, L, CP)
        key_float = key_proj.astype(jnp.float32)
        value_float = value_proj.astype(jnp.float32)

        def query_block(index):
            start = (index * KB).astype(jnp.int32)
            pair_rows = lax.dynamic_slice_in_dim(pair_full, start, KB, 0).astype(jnp.float32)
            pair_bias = jnp.einsum('qkc,ch->qhk', layer_norm(pair_rows, pair_gain), pair_proj, precision=lax.Precision.HIGHEST)
            query_rows = lax.dynamic_slice_in_dim(queries, start, KB, 1).astype(jnp.float32)
            scores = jnp.einsum('sqhd,skhd->qshk', query_rows, key_float) / math.sqrt(head_dim) + pair_bias[:, None]
            scores = jnp.where(key_live, scores, very_negative)
            row_peak = lax.optimization_barrier(jnp.max(scores, axis=-1, keepdims=True))
            soft_weights = jnp.exp(scores - row_peak)
            weighted = jnp.einsum('qshk,skhd->qshd', soft_weights, value_float, precision=lax.Precision.HIGHEST)
            return (weighted / lax.optimization_barrier(jnp.sum(soft_weights, axis=-1))[..., None]).reshape(KB, SAMPLES, D)
        attended = lax.map(query_block, jnp.arange(N_PB, dtype=jnp.int32))
        attended = attended.reshape(L, SAMPLES, D).transpose(1, 0, 2)
        gated_out = (attended * gate_vals.astype(jnp.float32)).astype(jnp.bfloat16).reshape(SAMPLES * L, D)
        mixed_rows = (group_single.astype(jnp.float32).reshape(SAMPLES * L, D) + project(gated_out, w_out)).astype(jnp.bfloat16)
        normed_t = layer_norm(mixed_rows.astype(jnp.float32), trans_gain).astype(jnp.bfloat16)
        hidden = (jax.nn.silu(project(normed_t, w_swish)) * project(normed_t, w_up)).astype(jnp.bfloat16)
        updated = (mixed_rows.astype(jnp.float32) + project(hidden, w_down)).astype(jnp.bfloat16)
        return updated.reshape(SAMPLES, L, D)
    return lax.map(one_group, (lengths, single, pair_rep))
```

```python
import functools
import math

import jax
import jax.numpy as jnp
from jax import lax
from jax.experimental import pallas as pl
from jax.experimental.pallas import tpu as pltpu
from jax.sharding import PartitionSpec as P

HEADS = 16
TP = 4

epsilon = 1e-05
very_negative = -1e30
f32 = jnp.float32
bf16 = jnp.bfloat16
VMEM_LIMIT = 48 * 1024 * 1024


def layer_norm(inputs, scale_gain):
    mean_val = jnp.mean(inputs, axis=-1, keepdims=True)
    centred = inputs - mean_val
    spread = jnp.mean(centred * centred, axis=-1, keepdims=True)
    return centred * lax.rsqrt(spread + epsilon) * scale_gain


def dot_last(a, b, precision=None):
    return lax.dot_general(
        a, b, (((1,), (1,)), ((), ())), preferred_element_type=f32, precision=precision
    )


def exchange(blocks, axes, groups=None):
    return lax.all_to_all(
        blocks, axes, split_axis=0, concat_axis=0, tiled=True, axis_index_groups=groups
    )


def spread(block, count, axes):
    return exchange(jnp.broadcast_to(block[None], (count,) + block.shape), axes)


def gather(block, axes):
    return lax.all_gather(block, axes, axis=0, tiled=False)


def swap(block, axis, flip):
    count = lax.axis_size(axis)
    return lax.ppermute(block, axis, [(i, i ^ flip) for i in range(count)])


def bias_kernel(info_ref, x_ref, gain_ref, proj_ref, *refs):
    out_refs, rows, held = refs[:-2], refs[-2], refs[-1]
    queries, keys, channels = x_ref.shape
    pairs = len(out_refs)
    normed = layer_norm(
        x_ref[...].reshape(queries * keys, channels).astype(f32), gain_ref[...]
    )
    rows[...] = normed
    together = 256 // queries
    for start in range(0, keys, together):
        block = jnp.concatenate(
            [rows[pl.ds(start + j, queries, stride=keys), :] for j in range(together)], axis=0
        )
        bias = dot_last(proj_ref[...], block, lax.Precision.HIGHEST)
        for j in range(together):
            cols = slice(j * queries, (j + 1) * queries)
            tile = jnp.concatenate([bias[:pairs, cols], bias[pairs:, cols]], axis=1)
            held[:, start + j, :] = tile
    for flip, out_ref in enumerate(out_refs):
        out_ref[...] = held[info_ref[1] ^ flip]


def attention_kernel(feats, info_ref, x_ref, other_ref, gain_ref, w_ref, *refs):
    count = len(refs) - 5
    bias_refs = refs[:count]
    out_ref, held_normed, held_bias, held_query, held_gate = refs[count:]
    places, own_rows, width = x_ref.shape
    chips = count // 2
    blocks = places // chips
    keys_held, lanes = bias_refs[0].shape
    q_rows = lanes // 2
    each = q_rows // count
    samples = own_rows // each
    key_count = blocks * q_rows
    head_dim = feats // 2
    length, at, block_at = info_ref[0], info_ref[1], info_ref[2]
    core = at % 2
    weights = w_ref[...].reshape(width, 4 * feats)
    w_kv, w_qg = weights[:, : 2 * feats], weights[:, 2 * feats :]
    key_value = []
    for side, ref in enumerate((x_ref, other_ref)):
        x = ref[...].reshape(places * own_rows, width).astype(f32)
        normed = layer_norm(x, gain_ref[...]).astype(bf16)
        held_normed[side] = normed.reshape(places, own_rows, width)
        proj = jnp.dot(normed, w_kv, preferred_element_type=f32)
        key_value.append(proj.reshape(places, samples, each, 2 * feats))
    for side in range(2):
        rows = held_normed[side, pl.ds(block_at * chips, chips)].reshape(chips * own_rows, width)
        proj = jnp.dot(rows, w_qg, preferred_element_type=f32)
        for z in range(chips):
            k = 2 * z + (core ^ side)
            part = proj[z * own_rows : (z + 1) * own_rows]
            held_query[k] = part[:, :feats]
            held_gate[k] = part[:, feats:]
    for flip in range(count):
        held_bias[at ^ flip] = bias_refs[flip][...]
    bias = jnp.concatenate(
        [
            held_bias[2 * z + (core ^ side), b * each : (b + 1) * each, :]
            for side in range(2)
            for b in range(blocks)
            for z in range(chips)
        ],
        axis=0,
    )
    index = lax.broadcasted_iota(jnp.int32, (key_count, lanes), 0)
    span = places * each
    side = index // span
    position = ((index % span) // each) * (2 * each) + (side ^ core) * each + index % each
    live = position < length
    first = lax.broadcasted_iota(jnp.int32, (q_rows, feats), 1) < head_dim
    done = []
    for s in range(samples):
        both_sides = jnp.concatenate(
            [part[:, s].reshape(span, 2 * feats) for part in key_value], axis=0
        )
        keys = both_sides[:, :feats].astype(bf16)
        values = both_sides[:, feats:].astype(bf16)
        rows = slice(s * each, (s + 1) * each)
        query = held_query[:, rows, :].reshape(q_rows, feats)
        both = jnp.concatenate(
            [jnp.where(first, query, 0.0), jnp.where(first, 0.0, query)], axis=0
        ).astype(bf16)
        scores = dot_last(keys, both) * (1.0 / math.sqrt(head_dim)) + bias
        scores = jnp.where(live, scores, very_negative)
        peak = jnp.max(scores, axis=0, keepdims=True)
        soft = jnp.exp(scores - peak)
        total = jnp.sum(soft, axis=0, keepdims=True)
        weighted = lax.dot_general(
            values, soft.astype(bf16), (((0,), (0,)), ((), ())), preferred_element_type=f32
        )
        attended = (weighted / total).T
        attended = jnp.where(first, attended[:q_rows], attended[q_rows:])
        gate = jax.nn.sigmoid(held_gate[:, rows, :].reshape(q_rows, feats))
        gate = gate.astype(bf16).astype(f32)
        done.append((attended * gate).reshape(count, each, feats))
        if s % 2:
            size = 2 * each
            start = s // 2 * size
            out_ref[:, start : start + size, :] = jnp.concatenate(done, axis=1).astype(bf16)
            done = []


def mix_kernel(
    info_ref, gated_ref, w_ref, other_ref, single_ref, gain_ref, mixed_ref, normed_ref, held
):
    ka_count, rows, feats = gated_ref.shape
    width = single_ref.shape[1]
    chips = ka_count // 2
    at = info_ref[1]
    gated = jnp.concatenate([gated_ref[k] for k in range(ka_count)], axis=1)
    for side, ref in enumerate((w_ref, other_ref)):
        weights = ref[:, :, ref.shape[2] - chips * feats :].reshape(width, chips * feats)
        added = jnp.dot(gated, weights, preferred_element_type=f32)
        for flip in range(chips):
            held[at ^ (2 * flip + side)] = added[:, flip * feats : (flip + 1) * feats]
    added = jnp.concatenate([held[k] for k in range(ka_count)], axis=1)
    mixed = (single_ref[...].astype(f32) + added).astype(bf16)
    mixed_ref[...] = mixed
    normed = layer_norm(mixed.astype(f32), gain_ref[...]).astype(bf16)
    for i in range(normed_ref.shape[0]):
        normed_ref[i] = normed


def transition_kernel(hidden_count, x_ref, w_ref, out_ref):
    groups, rows, width = x_ref.shape
    part = hidden_count
    x = x_ref[...].reshape(groups * rows, width)
    down, swish, up = (
        w_ref[:, :, i * part : (i + 1) * part].reshape(width, part) for i in range(3)
    )
    a = jnp.dot(x, swish, preferred_element_type=f32)
    b = jnp.dot(x, up, preferred_element_type=f32)
    hidden = ((a / (1.0 + jnp.exp(-a))) * b).astype(bf16)
    out_ref[...] = dot_last(hidden, down).astype(bf16).reshape(groups, rows, width)


def finish_kernel(mixed_ref, part_ref, out_ref):
    total = mixed_ref[...].astype(f32)
    for i in range(part_ref.shape[0]):
        total = total + part_ref[i].astype(f32)
    out_ref[...] = total.astype(bf16)


def call(kernel, out_shape, scratch=(), scalars=0, flops=0, moved=0):
    def run(*operands):
        return pl.pallas_call(
            kernel,
            out_shape=out_shape,
            in_specs=[
                pl.BlockSpec(memory_space=pltpu.SMEM if i < scalars else pltpu.VMEM)
                for i in range(len(operands))
            ],
            scratch_shapes=list(scratch),
            compiler_params=pltpu.CompilerParams(vmem_limit_bytes=VMEM_LIMIT),
            cost_estimate=pl.CostEstimate(flops=flops, bytes_accessed=moved, transcendentals=0),
        )(*operands)

    return run


def on_device(
    lengths,
    single,
    attn_gain,
    w_query,
    w_key,
    w_value,
    w_gate,
    w_out,
    pair_rep,
    pair_gain,
    pair_proj,
    trans_gain,
    w_swish,
    w_up,
    w_down,
):
    grp_count = lax.axis_size("grp")
    pb_count = lax.axis_size("pb")
    ka_count = lax.axis_size("ka")
    ka_index = lax.axis_index("ka")
    samples, row_count, width = single.shape[1:]
    w_rows = w_query.shape[0]
    feats = width // ka_count
    hid = w_swish.shape[1]
    own_rows = samples * row_count
    chips = ka_count // 2
    held = ka_count // TP
    info = jnp.stack([lengths[0], ka_index, lax.axis_index("pb")]).astype(jnp.int32)
    own = single.reshape(own_rows, width)

    line = [[i * 2 + c for i in range(pb_count * chips)] for c in range(2)]
    x = lax.all_gather(own, ("pb", "ka"), axis=0, tiled=False, axis_index_groups=line)
    other = swap(x, "ka", 1)

    early = [
        lax.dynamic_slice_in_dim(w, ka_index * feats, feats, 1)
        for w in (w_key, w_value, w_query, w_gate)
    ]
    early = jnp.concatenate(early + [w_down.T, w_swish, w_up, w_out], axis=1)
    early, pair_rep = lax.optimization_barrier((early, pair_rep))
    early = spread(early, pb_count, "pb").reshape(pb_count * w_rows, early.shape[1])

    attn_w = spread(early[:, : 4 * feats], grp_count, "grp")

    out_w = early[:, 4 * feats + 3 * hid :]
    out_w = [out_w] + [swap(out_w, "ka", 2)]
    late = jnp.concatenate([early[:, 4 * feats : 4 * feats + 3 * hid]] + out_w, axis=1)
    late = [late] + [swap(late, "ka", TP)]
    late = jnp.concatenate(
        [w[:, i * hid : (i + 1) * hid] for i in range(3) for w in late]
        + [w[:, 3 * hid :] for w in late],
        axis=1,
    )

    _, queries, key_blocks, key_rows, channels = pair_rep.shape
    keys_held = key_blocks * key_rows
    lanes = 2 * queries
    proj = pair_proj.reshape(channels, HEADS // 2, 2).transpose(2, 1, 0).reshape(HEADS, channels)
    bias = call(
        bias_kernel,
        (jax.ShapeDtypeStruct((keys_held, lanes), f32),) * ka_count,
        scratch=[
            pltpu.VMEM((queries * keys_held, channels), f32),
            pltpu.VMEM((ka_count, keys_held, lanes), f32),
        ],
        scalars=1,
        flops=2 * 6 * queries * keys_held * channels * HEADS,
        moved=queries * keys_held * channels * 2 + 4 * ka_count * keys_held * lanes,
    )(info, pair_rep.reshape(queries, keys_held, channels), pair_gain.reshape(1, channels), proj)
    late, attn_w, bias = lax.optimization_barrier((late, attn_w, list(bias)))
    late = spread(late, grp_count, "grp")
    bias = [bias[0]] + [swap(bias[i], "ka", i) for i in range(1, ka_count)]

    gated = call(
        functools.partial(attention_kernel, feats),
        jax.ShapeDtypeStruct((ka_count, own_rows, feats), bf16),
        scratch=[
            pltpu.VMEM((2,) + x.shape, bf16),
            pltpu.VMEM((ka_count, keys_held, lanes), f32),
            pltpu.VMEM((ka_count, own_rows, feats), f32),
            pltpu.VMEM((ka_count, own_rows, feats), f32),
        ],
        scalars=1,
        flops=4 * x.size * 2 * feats,
        moved=x.size * 4 + attn_w.size * 2,
    )(info, x, other, attn_gain.reshape(1, width), attn_w, *bias)
    gated = exchange(gated, "ka")
    out_w = swap(late[:, :, held * 3 * hid :], "ka", 1)

    rows = jax.ShapeDtypeStruct((own_rows, width), bf16)
    shared = jax.ShapeDtypeStruct((TP, own_rows, width), bf16)
    mixed, normed_t = call(
        mix_kernel,
        (rows, shared),
        scratch=[pltpu.VMEM((ka_count, own_rows, feats), f32)],
        scalars=1,
        flops=2 * own_rows * width * width,
        moved=width * width * 2,
    )(info, gated, late, out_w, own, trans_gain.reshape(1, width))

    groups = [list(range(i, i + TP)) for i in range(0, ka_count, TP)]
    normed_t = exchange(normed_t, "ka", groups)
    part = call(
        functools.partial(transition_kernel, held * hid),
        shared,
        flops=2 * own_rows * width * hid * ka_count * 3,
        moved=3 * width * hid * ka_count // TP * 2,
    )(normed_t, late)
    part = exchange(part, "ka", groups)
    result = call(finish_kernel, rows)(mixed, part)
    return result.reshape(1, samples, row_count, width)


def solution(mesh):
    return jax.shard_map(
        on_device,
        mesh=mesh,
        in_specs=(
            P("grp"),
            P("grp", None, ("pb", "ka"), None),
            P(),
            P(("grp", "pb"), None),
            P(("grp", "pb"), None),
            P(("grp", "pb"), None),
            P(("grp", "pb"), None),
            P(("grp", "pb"), "ka"),
            P("grp", "pb", None, "ka", None),
            P(),
            P(),
            P(),
            P(("grp", "pb"), "ka"),
            P(("grp", "pb"), "ka"),
            P("ka", ("grp", "pb")),
        ),
        out_specs=P("grp", None, ("pb", "ka"), None),
        check_vma=False,
    )
```

```python
import functools
import math

import jax
import jax.numpy as jnp
from jax import lax
from jax.experimental import pallas as pl
from jax.experimental.pallas import tpu as pltpu
from jax.sharding import PartitionSpec as P

HEADS = 16
TP = 4

epsilon = 1e-05
very_negative = -1e30
f32 = jnp.float32
bf16 = jnp.bfloat16
VMEM_LIMIT = 48 * 1024 * 1024
MOST_VMEM = 62 * 1024 * 1024


def layer_norm(inputs, scale_gain):
    mean_val = jnp.mean(inputs, axis=-1, keepdims=True)
    centred = inputs - mean_val
    spread = jnp.mean(centred * centred, axis=-1, keepdims=True)
    return centred * lax.rsqrt(spread + epsilon) * scale_gain


def dot_last(a, b, precision=None):
    return lax.dot_general(
        a, b, (((1,), (1,)), ((), ())), preferred_element_type=f32, precision=precision
    )


def exchange(blocks, axes, groups=None):
    return lax.all_to_all(
        blocks, axes, split_axis=0, concat_axis=0, tiled=True, axis_index_groups=groups
    )


def spread(block, count, axes):
    return exchange(jnp.broadcast_to(block[None], (count,) + block.shape), axes)


def gather(block, axes):
    return lax.all_gather(block, axes, axis=0, tiled=False)


def swap(block, axis, flip):
    count = lax.axis_size(axis)
    return lax.ppermute(block, axis, [(i, i ^ flip) for i in range(count)])


def bias_kernel(x_ref, gain_ref, proj_ref, *refs):
    out_refs, rows, held = refs[:-2], refs[-2], refs[-1]
    queries, keys, channels = x_ref.shape
    pairs = len(out_refs)
    normed = layer_norm(
        x_ref[...].reshape(queries * keys, channels).astype(f32), gain_ref[...].reshape(1, -1)
    )
    rows[...] = normed
    together = 256 // queries
    for start in range(0, keys, together):
        block = jnp.concatenate(
            [rows[pl.ds(start + j, queries, stride=keys), :] for j in range(together)], axis=0
        )
        bias = dot_last(proj_ref[...], block, lax.Precision.HIGHEST)
        for j in range(together):
            cols = slice(j * queries, (j + 1) * queries)
            tile = jnp.concatenate([bias[:pairs, cols], bias[pairs:, cols]], axis=1)
            held[:, start + j, :] = tile
    for flip, out_ref in enumerate(out_refs):
        out_ref[...] = held[lax.axis_index("ka") ^ flip]


def attention_kernel(feats, length_ref, x_ref, other_ref, gain_ref, w_ref, *refs):
    count = len(refs) - 5
    bias_refs = refs[:count]
    out_ref, held_normed, held_bias, held_query, held_gate = refs[count:]
    places, own_rows, width = x_ref.shape
    chips = count // 2
    blocks = places // chips
    keys_held, lanes = bias_refs[0].shape
    q_rows = lanes // 2
    each = q_rows // count
    samples = own_rows // each
    key_count = blocks * q_rows
    head_dim = feats // 2
    length, at, block_at = length_ref[0], lax.axis_index("ka"), lax.axis_index("pb")
    core = at % 2
    weights = w_ref[...].reshape(width, 4 * feats)
    w_kv, w_qg = weights[:, : 2 * feats], weights[:, 2 * feats :]
    key_value = []
    for side, ref in enumerate((x_ref, other_ref)):
        x = ref[...].reshape(places * own_rows, width).astype(f32)
        normed = layer_norm(x, gain_ref[...].reshape(1, -1)).astype(bf16)
        held_normed[side] = normed.reshape(places, own_rows, width)
        proj = jnp.dot(normed, w_kv, preferred_element_type=f32)
        key_value.append(proj.reshape(places, samples, each, 2 * feats))
    for side in range(2):
        rows = held_normed[side, pl.ds(block_at * chips, chips)].reshape(chips * own_rows, width)
        proj = jnp.dot(rows, w_qg, preferred_element_type=f32)
        for z in range(chips):
            k = 2 * z + (core ^ side)
            part = proj[z * own_rows : (z + 1) * own_rows]
            held_query[k] = part[:, :feats]
            held_gate[k] = part[:, feats:]
    for flip in range(count):
        held_bias[at ^ flip] = bias_refs[flip][...]
    bias = jnp.concatenate(
        [
            held_bias[2 * z + (core ^ side), b * each : (b + 1) * each, :]
            for side in range(2)
            for b in range(blocks)
            for z in range(chips)
        ],
        axis=0,
    )
    index = lax.broadcasted_iota(jnp.int32, (key_count, lanes), 0)
    span = places * each
    side = index // span
    position = ((index % span) // each) * (2 * each) + (side ^ core) * each + index % each
    live = position < length
    first = lax.broadcasted_iota(jnp.int32, (q_rows, feats), 1) < head_dim
    done = []
    for s in range(samples):
        both_sides = jnp.concatenate(
            [part[:, s].reshape(span, 2 * feats) for part in key_value], axis=0
        )
        keys = both_sides[:, :feats].astype(bf16)
        values = both_sides[:, feats:].astype(bf16)
        rows = slice(s * each, (s + 1) * each)
        query = held_query[:, rows, :].reshape(q_rows, feats)
        both = jnp.concatenate(
            [jnp.where(first, query, 0.0), jnp.where(first, 0.0, query)], axis=0
        ).astype(bf16)
        scores = dot_last(keys, both) * (1.0 / math.sqrt(head_dim)) + bias
        scores = jnp.where(live, scores, very_negative)
        peak = jnp.max(scores, axis=0, keepdims=True)
        soft = jnp.exp(scores - peak)
        total = jnp.sum(soft, axis=0, keepdims=True)
        weighted = lax.dot_general(
            values, soft.astype(bf16), (((0,), (0,)), ((), ())), preferred_element_type=f32
        )
        attended = (weighted / total).T
        attended = jnp.where(first, attended[:q_rows], attended[q_rows:])
        gate = jax.nn.sigmoid(held_gate[:, rows, :].reshape(q_rows, feats))
        gate = gate.astype(bf16).astype(f32)
        done.append((attended * gate).reshape(count, each, feats))
        if s % 2:
            size = 2 * each
            start = s // 2 * size
            out_ref[:, start : start + size, :] = jnp.concatenate(done, axis=1).astype(bf16)
            done = []


def mix_kernel(
    gated_ref, w_ref, other_ref, single_ref, gain_ref, mixed_ref, normed_ref, held
):
    ka_count, rows, feats = gated_ref.shape
    width = single_ref.shape[1]
    chips = ka_count // 2
    at = lax.axis_index("ka")
    gated = jnp.concatenate([gated_ref[k] for k in range(ka_count)], axis=1)
    for side, ref in enumerate((w_ref, other_ref)):
        weights = ref[:, :, ref.shape[2] - chips * feats :].reshape(width, chips * feats)
        added = jnp.dot(gated, weights, preferred_element_type=f32)
        for flip in range(chips):
            held[at ^ (2 * flip + side)] = added[:, flip * feats : (flip + 1) * feats]
    added = jnp.concatenate([held[k] for k in range(ka_count)], axis=1)
    mixed = (single_ref[...].astype(f32) + added).astype(bf16)
    mixed_ref[...] = mixed
    normed = layer_norm(mixed.astype(f32), gain_ref[...].reshape(1, -1)).astype(bf16)
    for i in range(normed_ref.shape[0]):
        normed_ref[i] = normed


def transition_kernel(hidden_count, x_ref, w_ref, out_ref):
    groups, rows, width = x_ref.shape
    part = hidden_count
    x = x_ref[...].reshape(groups * rows, width)
    down, swish, up = (
        w_ref[:, :, i * part : (i + 1) * part].reshape(width, part) for i in range(3)
    )
    a = jnp.dot(x, swish, preferred_element_type=f32)
    b = jnp.dot(x, up, preferred_element_type=f32)
    hidden = ((a / (1.0 + jnp.exp(-a))) * b).astype(bf16)
    out_ref[...] = dot_last(hidden, down).astype(bf16).reshape(groups, rows, width)


def finish_kernel(mixed_ref, part_ref, out_ref):
    total = mixed_ref[...].astype(f32)
    for i in range(part_ref.shape[0]):
        total = total + part_ref[i].astype(f32)
    out_ref[...] = total.astype(bf16)


def call(kernel, out_shape, scratch=(), scalars=0, flops=0, moved=0, limit=VMEM_LIMIT):
    def run(*operands):
        return pl.pallas_call(
            kernel,
            out_shape=out_shape,
            in_specs=[
                pl.BlockSpec(memory_space=pltpu.SMEM if i < scalars else pltpu.VMEM)
                for i in range(len(operands))
            ],
            scratch_shapes=list(scratch),
            compiler_params=pltpu.CompilerParams(vmem_limit_bytes=limit),
            cost_estimate=pl.CostEstimate(flops=flops, bytes_accessed=moved, transcendentals=0),
        )(*operands)

    return run


def on_device(
    lengths,
    single,
    attn_gain,
    w_query,
    w_key,
    w_value,
    w_gate,
    w_out,
    pair_rep,
    pair_gain,
    pair_proj,
    trans_gain,
    w_swish,
    w_up,
    w_down,
):
    grp_count = lax.axis_size("grp")
    pb_count = lax.axis_size("pb")
    ka_count = lax.axis_size("ka")
    ka_index = lax.axis_index("ka")
    samples, row_count, width = single.shape[1:]
    w_rows = w_query.shape[0]
    feats = width // ka_count
    hid = w_swish.shape[1]
    own_rows = samples * row_count
    chips = ka_count // 2
    held = ka_count // TP
    own = single.reshape(own_rows, width)

    line = [[i * 2 + c for i in range(pb_count * chips)] for c in range(2)]
    x = lax.all_gather(own, ("pb", "ka"), axis=0, tiled=False, axis_index_groups=line)

    early = [
        lax.dynamic_slice_in_dim(w, ka_index * feats, feats, 1)
        for w in (w_key, w_value, w_query, w_gate)
    ]
    early = jnp.concatenate(early + [w_down.T, w_swish, w_up, w_out], axis=1)
    early, pair_rep = lax.optimization_barrier((early, pair_rep))
    early = spread(early, pb_count, "pb")

    _, queries, key_blocks, key_rows, channels = pair_rep.shape
    keys_held = key_blocks * key_rows
    lanes = 2 * queries
    proj = pair_proj.reshape(channels, HEADS // 2, 2).transpose(2, 1, 0).reshape(HEADS, channels)
    bias = call(
        bias_kernel,
        (jax.ShapeDtypeStruct((keys_held, lanes), f32),) * ka_count,
        scratch=[
            pltpu.VMEM((queries * keys_held, channels), f32),
            pltpu.VMEM((ka_count, keys_held, lanes), f32),
        ],
        flops=2 * 6 * queries * keys_held * channels * HEADS,
        moved=queries * keys_held * channels * 2 + 4 * ka_count * keys_held * lanes,
    )(pair_rep.reshape(queries, keys_held, channels), pair_gain, proj)
    near = [swap(bias[i], "ka", i) for i in (1, 2)]
    early, near = lax.optimization_barrier((early, near))
    early = early.reshape(pb_count * w_rows, early.shape[2])

    attn_w = spread(early[:, : 4 * feats], grp_count, "grp")

    out_w = early[:, 4 * feats + 3 * hid :]
    out_w = [out_w] + [swap(out_w, "ka", 2)]
    late = jnp.concatenate([early[:, 4 * feats : 4 * feats + 3 * hid]] + out_w, axis=1)
    late = [late] + [swap(late, "ka", TP)]
    late = jnp.concatenate(
        [w[:, i * hid : (i + 1) * hid] for i in range(3) for w in late]
        + [w[:, 3 * hid :] for w in late],
        axis=1,
    )

    late, attn_w, far = lax.optimization_barrier((late, attn_w, list(bias[3:])))
    late = spread(late, grp_count, "grp")
    far = [swap(block, "ka", i + 3) for i, block in enumerate(far)]
    x, far = lax.optimization_barrier((x, far))
    other = swap(x, "ka", 1)
    bias = [bias[0]] + near + far

    gated = call(
        functools.partial(attention_kernel, feats),
        jax.ShapeDtypeStruct((ka_count, own_rows, feats), bf16),
        scratch=[
            pltpu.VMEM((2,) + x.shape, bf16),
            pltpu.VMEM((ka_count, keys_held, lanes), f32),
            pltpu.VMEM((ka_count, own_rows, feats), f32),
            pltpu.VMEM((ka_count, own_rows, feats), f32),
        ],
        scalars=1,
        flops=4 * x.size * 2 * feats,
        moved=x.size * 4 + attn_w.size * 2,
        limit=MOST_VMEM,
    )(lengths, x, other, attn_gain, attn_w, *bias)
    gated, late = lax.optimization_barrier((gated, late))
    gated = exchange(gated, "ka")
    out_w = swap(late[:, :, held * 3 * hid :], "ka", 1)

    rows = jax.ShapeDtypeStruct((own_rows, width), bf16)
    shared = jax.ShapeDtypeStruct((TP, own_rows, width), bf16)
    mixed, normed_t = call(
        mix_kernel,
        (rows, shared),
        scratch=[pltpu.VMEM((ka_count, own_rows, feats), f32)],
        flops=2 * own_rows * width * width,
        moved=width * width * 2,
    )(gated, late, out_w, own, trans_gain)

    groups = [list(range(i, i + TP)) for i in range(0, ka_count, TP)]
    normed_t = exchange(normed_t, "ka", groups)
    part = call(
        functools.partial(transition_kernel, held * hid),
        shared,
        flops=2 * own_rows * width * hid * ka_count * 3,
        moved=3 * width * hid * ka_count // TP * 2,
    )(normed_t, late)
    part = exchange(part, "ka", groups)
    result = call(finish_kernel, rows)(mixed, part)
    return result.reshape(1, samples, row_count, width)


def solution(mesh):
    return jax.shard_map(
        on_device,
        mesh=mesh,
        in_specs=(
            P("grp"),
            P("grp", None, ("pb", "ka"), None),
            P(),
            P(("grp", "pb"), None),
            P(("grp", "pb"), None),
            P(("grp", "pb"), None),
            P(("grp", "pb"), None),
            P(("grp", "pb"), "ka"),
            P("grp", "pb", None, "ka", None),
            P(),
            P(),
            P(),
            P(("grp", "pb"), "ka"),
            P(("grp", "pb"), "ka"),
            P("ka", ("grp", "pb")),
        ),
        out_specs=P("grp", None, ("pb", "ka"), None),
        check_vma=False,
    )
```

```python
import functools
import math

import jax
import jax.numpy as jnp
from jax import lax
from jax.experimental import pallas as pl
from jax.experimental.pallas import tpu as pltpu
from jax.sharding import PartitionSpec as P

HEADS = 16
TP = 4

epsilon = 1e-05
very_negative = -1e30
f32 = jnp.float32
bf16 = jnp.bfloat16
VMEM_LIMIT = 48 * 1024 * 1024
MOST_VMEM = 63 * 1024 * 1024


def layer_norm(inputs, scale_gain):
    mean_val = jnp.mean(inputs, axis=-1, keepdims=True)
    centred = inputs - mean_val
    spread = jnp.mean(centred * centred, axis=-1, keepdims=True)
    return centred * lax.rsqrt(spread + epsilon) * scale_gain


def dot_last(a, b, precision=None):
    return lax.dot_general(
        a, b, (((1,), (1,)), ((), ())), preferred_element_type=f32, precision=precision
    )


def exchange(blocks, axes, groups=None):
    return lax.all_to_all(
        blocks, axes, split_axis=0, concat_axis=0, tiled=True, axis_index_groups=groups
    )


def spread(block, count, axes):
    return exchange(jnp.broadcast_to(block[None], (count,) + block.shape), axes)


def gather(block, axes):
    return lax.all_gather(block, axes, axis=0, tiled=False)


def swap(block, axis, flip):
    count = lax.axis_size(axis)
    return lax.ppermute(block, axis, [(i, i ^ flip) for i in range(count)])


def bias_kernel(x_ref, gain_ref, proj_ref, *refs):
    out_refs, rows, held = refs[:-2], refs[-2], refs[-1]
    queries, keys, channels = x_ref.shape
    pairs = len(out_refs)
    normed = layer_norm(
        x_ref[...].reshape(queries * keys, channels).astype(f32), gain_ref[...].reshape(1, -1)
    )
    rows[...] = normed
    together = 256 // queries
    for start in range(0, keys, together):
        block = jnp.concatenate(
            [rows[pl.ds(start + j, queries, stride=keys), :] for j in range(together)], axis=0
        )
        bias = dot_last(proj_ref[...], block, lax.Precision.HIGHEST)
        for j in range(together):
            cols = slice(j * queries, (j + 1) * queries)
            tile = jnp.concatenate([bias[:pairs, cols], bias[pairs:, cols]], axis=1)
            held[:, start + j, :] = tile
    for flip, out_ref in enumerate(out_refs):
        out_ref[...] = held[lax.axis_index("ka") ^ flip]


def project_side(samples, x_ref, gain_ref, w_ref, held_ref, kv_ref):
    places, own_rows, width = x_ref.shape
    feats = kv_ref.shape[2] // 2
    each = own_rows // samples
    chips = places // lax.axis_size("pb")
    weights = w_ref[...].reshape(width, 4 * feats)
    x = x_ref[...].reshape(places * own_rows, width).astype(f32)
    normed = layer_norm(x, gain_ref[...].reshape(1, -1)).astype(bf16)
    held_ref[...] = normed.reshape(places, own_rows, width)
    proj = jnp.dot(normed, weights[:, : 2 * feats], preferred_element_type=f32)
    proj = proj.reshape(places, samples, each, 2 * feats)
    for s in range(samples):
        kv_ref[s] = proj[:, s].reshape(places * each, 2 * feats).astype(bf16)
    rows = held_ref[pl.ds(lax.axis_index("pb") * chips, chips)].reshape(chips * own_rows, width)
    return jnp.dot(rows, weights[:, 2 * feats :], preferred_element_type=f32)


def project_kernel(x_ref, gain_ref, w_ref, kv_ref, query_ref, held_ref):
    samples = kv_ref.shape[0]
    query_ref[...] = project_side(samples, x_ref, gain_ref, w_ref, held_ref, kv_ref)


def attention_kernel(length_ref, x_ref, gain_ref, w_ref, kv_ref, near_ref, *refs):
    count = len(refs) - 6
    bias_refs = refs[:count]
    out_ref, held_normed, held_kv, held_bias, held_query, held_gate = refs[count:]
    places, own_rows, width = x_ref.shape
    samples, span, feats = kv_ref.shape
    feats = feats // 2
    chips = count // 2
    blocks = places // chips
    keys_held, lanes = bias_refs[0].shape
    q_rows = lanes // 2
    each = q_rows // count
    key_count = blocks * q_rows
    head_dim = feats // 2
    length, at = length_ref[0], lax.axis_index("ka")
    core = at % 2
    far = project_side(samples, x_ref, gain_ref, w_ref, held_normed, held_kv)
    for side, proj in enumerate((near_ref[...], far)):
        for z in range(chips):
            k = 2 * z + (core ^ side)
            part = proj[z * own_rows : (z + 1) * own_rows]
            held_query[k] = part[:, :feats]
            held_gate[k] = part[:, feats:]
    for flip in range(count):
        held_bias[at ^ flip] = bias_refs[flip][...]
    bias = jnp.concatenate(
        [
            held_bias[2 * z + (core ^ side), b * each : (b + 1) * each, :]
            for side in range(2)
            for b in range(blocks)
            for z in range(chips)
        ],
        axis=0,
    )
    index = lax.broadcasted_iota(jnp.int32, (key_count, lanes), 0)
    side = index // span
    position = ((index % span) // each) * (2 * each) + (side ^ core) * each + index % each
    live = position < length
    first = lax.broadcasted_iota(jnp.int32, (q_rows, feats), 1) < head_dim
    done = []
    for s in range(samples):
        both_sides = jnp.concatenate([kv_ref[s], held_kv[s]], axis=0)
        keys, values = both_sides[:, :feats], both_sides[:, feats:]
        rows = slice(s * each, (s + 1) * each)
        query = held_query[:, rows, :].reshape(q_rows, feats)
        both = jnp.concatenate(
            [jnp.where(first, query, 0.0), jnp.where(first, 0.0, query)], axis=0
        ).astype(bf16)
        scores = dot_last(keys, both) * (1.0 / math.sqrt(head_dim)) + bias
        scores = jnp.where(live, scores, very_negative)
        peak = jnp.max(scores, axis=0, keepdims=True)
        soft = jnp.exp(scores - peak)
        total = jnp.sum(soft, axis=0, keepdims=True)
        weighted = lax.dot_general(
            values, soft.astype(bf16), (((0,), (0,)), ((), ())), preferred_element_type=f32
        )
        attended = (weighted / total).T
        attended = jnp.where(first, attended[:q_rows], attended[q_rows:])
        gate = jax.nn.sigmoid(held_gate[:, rows, :].reshape(q_rows, feats))
        gate = gate.astype(bf16).astype(f32)
        done.append((attended * gate).reshape(count, each, feats))
        if s % 2:
            size = 2 * each
            start = s // 2 * size
            out_ref[:, start : start + size, :] = jnp.concatenate(done, axis=1).astype(bf16)
            done = []


def mix_kernel(
    gated_ref, w_ref, other_ref, single_ref, gain_ref, mixed_ref, normed_ref, held
):
    ka_count, rows, feats = gated_ref.shape
    width = single_ref.shape[1]
    chips = ka_count // 2
    at = lax.axis_index("ka")
    gated = jnp.concatenate([gated_ref[k] for k in range(ka_count)], axis=1)
    for side, ref in enumerate((w_ref, other_ref)):
        weights = ref[...].reshape(width, chips * feats)
        added = jnp.dot(gated, weights, preferred_element_type=f32)
        for flip in range(chips):
            held[at ^ (2 * flip + side)] = added[:, flip * feats : (flip + 1) * feats]
    added = jnp.concatenate([held[k] for k in range(ka_count)], axis=1)
    mixed = (single_ref[...].astype(f32) + added).astype(bf16)
    mixed_ref[...] = mixed
    normed = layer_norm(mixed.astype(f32), gain_ref[...].reshape(1, -1)).astype(bf16)
    for i in range(normed_ref.shape[0]):
        normed_ref[i] = normed


def transition_kernel(x_ref, w_ref, out_ref, swish, up, down, sems):
    groups, rows, width = x_ref.shape
    hidden_count = down.shape[2]
    copies = [
        pltpu.make_async_copy(
            w_ref.at[:, :, pl.ds(i * hidden_count, hidden_count)], part, sems.at[i]
        )
        for i, part in ((1, swish), (2, up), (0, down))
    ]
    for copy in copies:
        copy.start()
    x = x_ref[...].reshape(groups * rows, width)
    copies[0].wait()
    a = jnp.dot(x, swish[...].reshape(width, hidden_count), preferred_element_type=f32)
    copies[1].wait()
    b = jnp.dot(x, up[...].reshape(width, hidden_count), preferred_element_type=f32)
    hidden = ((a / (1.0 + jnp.exp(-a))) * b).astype(bf16)
    copies[2].wait()
    out = dot_last(hidden, down[...].reshape(width, hidden_count))
    out_ref[...] = out.astype(bf16).reshape(groups, rows, width)


def finish_kernel(mixed_ref, part_ref, out_ref):
    total = mixed_ref[...].astype(f32)
    for i in range(part_ref.shape[0]):
        total = total + part_ref[i].astype(f32)
    out_ref[...] = total.astype(bf16)


def call(kernel, out_shape, scratch=(), scalars=0, flops=0, moved=0, limit=VMEM_LIMIT, left=()):
    def run(*operands):
        return pl.pallas_call(
            kernel,
            out_shape=out_shape,
            in_specs=[
                pl.BlockSpec(
                    memory_space=pltpu.SMEM if i < scalars else pl.ANY if i in left else pltpu.VMEM
                )
                for i in range(len(operands))
            ],
            scratch_shapes=list(scratch),
            compiler_params=pltpu.CompilerParams(vmem_limit_bytes=limit),
            cost_estimate=pl.CostEstimate(flops=flops, bytes_accessed=moved, transcendentals=0),
        )(*operands)

    return run


def on_device(
    lengths,
    single,
    attn_gain,
    w_query,
    w_key,
    w_value,
    w_gate,
    w_out,
    pair_rep,
    pair_gain,
    pair_proj,
    trans_gain,
    w_swish,
    w_up,
    w_down,
):
    grp_count = lax.axis_size("grp")
    pb_count = lax.axis_size("pb")
    ka_count = lax.axis_size("ka")
    ka_index = lax.axis_index("ka")
    samples, row_count, width = single.shape[1:]
    w_rows = w_query.shape[0]
    feats = width // ka_count
    hid = w_swish.shape[1]
    own_rows = samples * row_count
    chips = ka_count // 2
    held = ka_count // TP
    own = single.reshape(own_rows, width)

    line = [[i * 2 + c for i in range(pb_count * chips)] for c in range(2)]
    x = lax.all_gather(own, ("pb", "ka"), axis=0, tiled=False, axis_index_groups=line)

    early = [
        lax.dynamic_slice_in_dim(w, ka_index * feats, feats, 1)
        for w in (w_key, w_value, w_query, w_gate)
    ]
    early = jnp.concatenate(early + [w_down.T, w_swish, w_up, w_out], axis=1)
    early, pair_rep = lax.optimization_barrier((early, pair_rep))
    early = spread(early, pb_count, "pb")

    _, queries, key_blocks, key_rows, channels = pair_rep.shape
    keys_held = key_blocks * key_rows
    lanes = 2 * queries
    proj = pair_proj.reshape(channels, HEADS // 2, 2).transpose(2, 1, 0).reshape(HEADS, channels)
    bias = call(
        bias_kernel,
        (jax.ShapeDtypeStruct((keys_held, lanes), f32),) * ka_count,
        scratch=[
            pltpu.VMEM((queries * keys_held, channels), f32),
            pltpu.VMEM((ka_count, keys_held, lanes), f32),
        ],
        flops=2 * 6 * queries * keys_held * channels * HEADS,
        moved=queries * keys_held * channels * 2 + 4 * ka_count * keys_held * lanes,
    )(pair_rep.reshape(queries, keys_held, channels), pair_gain, proj)
    near = [swap(bias[i], "ka", i) for i in (1, 2, 3)]
    early, near = lax.optimization_barrier((early, near))
    early = early.reshape(pb_count * w_rows, early.shape[2])

    attn_w = spread(early[:, : 4 * feats], grp_count, "grp")

    out_w = early[:, 4 * feats + 3 * hid :]
    out_w = [out_w] + [swap(out_w, "ka", 2)]
    late = jnp.concatenate([early[:, 4 * feats : 4 * feats + 3 * hid]] + out_w, axis=1)
    late = [late] + [swap(late, "ka", TP)]
    late = jnp.concatenate(
        [w[:, i * hid : (i + 1) * hid] for i in range(3) for w in late]
        + [w[:, 3 * hid :] for w in late],
        axis=1,
    )

    late, attn_w, far = lax.optimization_barrier((late, attn_w, list(bias[4:])))
    late = spread(late, grp_count, "grp")
    far = [swap(block, "ka", i + 4) for i, block in enumerate(far)]
    x, far = lax.optimization_barrier((x, far))
    other = swap(x, "ka", 1)
    bias = [bias[0]] + near + far

    line_rows = pb_count * chips * row_count
    kv_shape = (samples, line_rows, 2 * feats)
    query_shape = (chips * own_rows, 2 * feats)
    costs = dict(
        flops=2 * x.size * 3 * feats, moved=x.size * 2 + attn_w.size * 2, limit=MOST_VMEM
    )
    near_kv, near_query = call(
        project_kernel,
        (jax.ShapeDtypeStruct(kv_shape, bf16), jax.ShapeDtypeStruct(query_shape, f32)),
        scratch=[pltpu.VMEM(x.shape, bf16)],
        **costs,
    )(x, attn_gain, attn_w)
    gated = call(
        attention_kernel,
        jax.ShapeDtypeStruct((ka_count, own_rows, feats), bf16),
        scratch=[
            pltpu.VMEM(x.shape, bf16),
            pltpu.VMEM(kv_shape, bf16),
            pltpu.VMEM((ka_count, keys_held, lanes), f32),
            pltpu.VMEM((ka_count, own_rows, feats), f32),
            pltpu.VMEM((ka_count, own_rows, feats), f32),
        ],
        scalars=1,
        **costs,
    )(lengths, other, attn_gain, attn_w, near_kv, near_query, *bias)
    gated, late = lax.optimization_barrier((gated, late))
    gated = exchange(gated, "ka")
    out_w = late[:, :, held * 3 * hid :]
    other_w = swap(out_w, "ka", 1)

    rows = jax.ShapeDtypeStruct((own_rows, width), bf16)
    shared = jax.ShapeDtypeStruct((TP, own_rows, width), bf16)
    mixed, normed_t = call(
        mix_kernel,
        (rows, shared),
        scratch=[pltpu.VMEM((ka_count, own_rows, feats), f32)],
        flops=2 * own_rows * width * width,
        moved=width * width * 2,
    )(gated, out_w, other_w, own, trans_gain)

    groups = [list(range(i, i + TP)) for i in range(0, ka_count, TP)]
    normed_t = exchange(normed_t, "ka", groups)
    part = call(
        transition_kernel,
        shared,
        scratch=[pltpu.VMEM((grp_count, pb_count * w_rows, held * hid), bf16)] * 3
        + [pltpu.SemaphoreType.DMA((3,))],
        left=(1,),
        flops=2 * own_rows * width * hid * ka_count * 3,
        moved=3 * width * hid * ka_count // TP * 2,
    )(normed_t, late)
    part = exchange(part, "ka", groups)
    result = call(finish_kernel, rows)(mixed, part)
    return result.reshape(1, samples, row_count, width)


def solution(mesh):
    return jax.shard_map(
        on_device,
        mesh=mesh,
        in_specs=(
            P("grp"),
            P("grp", None, ("pb", "ka"), None),
            P(),
            P(("grp", "pb"), None),
            P(("grp", "pb"), None),
            P(("grp", "pb"), None),
            P(("grp", "pb"), None),
            P(("grp", "pb"), "ka"),
            P("grp", "pb", None, "ka", None),
            P(),
            P(),
            P(),
            P(("grp", "pb"), "ka"),
            P(("grp", "pb"), "ka"),
            P("ka", ("grp", "pb")),
        ),
        out_specs=P("grp", None, ("pb", "ka"), None),
        check_vma=False,
    )
```

```python
import functools
import math

import jax
import jax.numpy as jnp
from jax import lax
from jax.experimental import pallas as pl
from jax.experimental.pallas import tpu as pltpu
from jax.sharding import PartitionSpec as P

HEADS = 16
TP = 4

epsilon = 1e-05
very_negative = -1e30
f32 = jnp.float32
bf16 = jnp.bfloat16
VMEM_LIMIT = 48 * 1024 * 1024
MOST_VMEM = 63 * 1024 * 1024


def layer_norm(inputs, scale_gain):
    mean_val = jnp.mean(inputs, axis=-1, keepdims=True)
    centred = inputs - mean_val
    spread = jnp.mean(centred * centred, axis=-1, keepdims=True)
    return centred * lax.rsqrt(spread + epsilon) * scale_gain


def dot_last(a, b, precision=None):
    return lax.dot_general(
        a, b, (((1,), (1,)), ((), ())), preferred_element_type=f32, precision=precision
    )


def exchange(blocks, axes, groups=None):
    return lax.all_to_all(
        blocks, axes, split_axis=0, concat_axis=0, tiled=True, axis_index_groups=groups
    )


def spread(block, count, axes):
    return exchange(jnp.broadcast_to(block[None], (count,) + block.shape), axes)


def gather(block, axes):
    return lax.all_gather(block, axes, axis=0, tiled=False)


def swap(block, axis, flip):
    count = lax.axis_size(axis)
    return lax.ppermute(block, axis, [(i, i ^ flip) for i in range(count)])


def bias_kernel(x_ref, gain_ref, proj_ref, *refs):
    out_refs, rows, held = refs[:-2], refs[-2], refs[-1]
    queries, keys, channels = x_ref.shape
    pairs = len(out_refs)
    normed = layer_norm(
        x_ref[...].reshape(queries * keys, channels).astype(f32), gain_ref[...].reshape(1, -1)
    )
    rows[...] = normed
    together = 256 // queries
    for start in range(0, keys, together):
        block = jnp.concatenate(
            [rows[pl.ds(start + j, queries, stride=keys), :] for j in range(together)], axis=0
        )
        bias = dot_last(proj_ref[...], block, lax.Precision.HIGHEST)
        for j in range(together):
            cols = slice(j * queries, (j + 1) * queries)
            tile = jnp.concatenate([bias[:pairs, cols], bias[pairs:, cols]], axis=1)
            held[:, start + j, :] = tile
    for flip, out_ref in enumerate(out_refs):
        out_ref[...] = held[lax.axis_index("ka") ^ flip]


def project_side(samples, x_ref, gain_ref, w_ref, raw_ref, held_ref, sems, kv_ref):
    places, own_rows, width = x_ref.shape
    feats = kv_ref.shape[2] // 2
    each = own_rows // samples
    blocks = lax.axis_size("pb")
    chips = places // blocks
    copies = [
        pltpu.make_async_copy(
            x_ref.at[pl.ds(b * chips, chips)], raw_ref.at[pl.ds(b * chips, chips)], sems.at[b]
        )
        for b in range(blocks)
    ]
    for copy in copies:
        copy.start()
    weights = w_ref[...].reshape(width, 4 * feats)
    for b, copy in enumerate(copies):
        copy.wait()
        part = slice(b * chips, (b + 1) * chips)
        x = raw_ref[part].reshape(chips * own_rows, width).astype(f32)
        normed = layer_norm(x, gain_ref[...].reshape(1, -1)).astype(bf16)
        held_ref[part] = normed.reshape(chips, own_rows, width)
        proj = jnp.dot(normed, weights[:, : 2 * feats], preferred_element_type=f32)
        proj = proj.reshape(chips, samples, each, 2 * feats)
        rows = slice(b * chips * each, (b + 1) * chips * each)
        for s in range(samples):
            kv_ref[s, rows] = proj[:, s].reshape(chips * each, 2 * feats).astype(bf16)
    rows = held_ref[pl.ds(lax.axis_index("pb") * chips, chips)].reshape(chips * own_rows, width)
    return jnp.dot(rows, weights[:, 2 * feats :], preferred_element_type=f32)


def project_kernel(x_ref, gain_ref, w_ref, kv_ref, query_ref, raw_ref, held_ref, sems):
    samples = kv_ref.shape[0]
    query_ref[...] = project_side(
        samples, x_ref, gain_ref, w_ref, raw_ref, held_ref, sems, kv_ref
    )


def attention_kernel(length_ref, x_ref, gain_ref, w_ref, kv_ref, near_ref, *refs):
    count = len(refs) - 8
    bias_refs = refs[:count]
    out_ref, raw, held_normed, sems, held_kv, held_bias, held_query, held_gate = refs[count:]
    places, own_rows, width = x_ref.shape
    samples, span, feats = kv_ref.shape
    feats = feats // 2
    chips = count // 2
    blocks = places // chips
    keys_held, lanes = bias_refs[0].shape
    q_rows = lanes // 2
    each = q_rows // count
    key_count = blocks * q_rows
    head_dim = feats // 2
    length, at = length_ref[0], lax.axis_index("ka")
    core = at % 2
    far = project_side(samples, x_ref, gain_ref, w_ref, raw, held_normed, sems, held_kv)
    for side, proj in enumerate((near_ref[...], far)):
        for z in range(chips):
            k = 2 * z + (core ^ side)
            part = proj[z * own_rows : (z + 1) * own_rows]
            held_query[k] = part[:, :feats]
            held_gate[k] = part[:, feats:]
    for flip in range(count):
        held_bias[at ^ flip] = bias_refs[flip][...]
    bias = jnp.concatenate(
        [
            held_bias[2 * z + (core ^ side), b * each : (b + 1) * each, :]
            for side in range(2)
            for b in range(blocks)
            for z in range(chips)
        ],
        axis=0,
    )
    index = lax.broadcasted_iota(jnp.int32, (key_count, lanes), 0)
    side = index // span
    position = ((index % span) // each) * (2 * each) + (side ^ core) * each + index % each
    live = position < length
    first = lax.broadcasted_iota(jnp.int32, (q_rows, feats), 1) < head_dim
    done = []
    for s in range(samples):
        both_sides = jnp.concatenate([kv_ref[s], held_kv[s]], axis=0)
        keys, values = both_sides[:, :feats], both_sides[:, feats:]
        rows = slice(s * each, (s + 1) * each)
        query = held_query[:, rows, :].reshape(q_rows, feats)
        both = jnp.concatenate(
            [jnp.where(first, query, 0.0), jnp.where(first, 0.0, query)], axis=0
        ).astype(bf16)
        scores = dot_last(keys, both) * (1.0 / math.sqrt(head_dim)) + bias
        scores = jnp.where(live, scores, very_negative)
        peak = jnp.max(scores, axis=0, keepdims=True)
        soft = jnp.exp(scores - peak)
        total = jnp.sum(soft, axis=0, keepdims=True)
        weighted = lax.dot_general(
            values, soft.astype(bf16), (((0,), (0,)), ((), ())), preferred_element_type=f32
        )
        attended = (weighted / total).T
        attended = jnp.where(first, attended[:q_rows], attended[q_rows:])
        gate = jax.nn.sigmoid(held_gate[:, rows, :].reshape(q_rows, feats))
        gate = gate.astype(bf16).astype(f32)
        done.append((attended * gate).reshape(count, each, feats))
        if s % 2:
            size = 2 * each
            start = s // 2 * size
            out_ref[:, start : start + size, :] = jnp.concatenate(done, axis=1).astype(bf16)
            done = []


def mix_kernel(
    gated_ref, w_ref, other_ref, single_ref, gain_ref, mixed_ref, normed_ref, held
):
    ka_count, rows, feats = gated_ref.shape
    width = single_ref.shape[1]
    chips = ka_count // 2
    at = lax.axis_index("ka")
    gated = jnp.concatenate([gated_ref[k] for k in range(ka_count)], axis=1)
    for side, ref in enumerate((w_ref, other_ref)):
        weights = ref[...].reshape(width, chips * feats)
        added = jnp.dot(gated, weights, preferred_element_type=f32)
        for flip in range(chips):
            held[at ^ (2 * flip + side)] = added[:, flip * feats : (flip + 1) * feats]
    added = jnp.concatenate([held[k] for k in range(ka_count)], axis=1)
    mixed = (single_ref[...].astype(f32) + added).astype(bf16)
    mixed_ref[...] = mixed
    normed = layer_norm(mixed.astype(f32), gain_ref[...].reshape(1, -1)).astype(bf16)
    normed_ref[...] = normed


def transition_kernel(x_ref, w_ref, out_ref, swish, up, down, sems):
    groups, rows, width = x_ref.shape
    hidden_count = down.shape[2]
    copies = [
        pltpu.make_async_copy(
            w_ref.at[:, :, pl.ds(i * hidden_count, hidden_count)], part, sems.at[i]
        )
        for i, part in ((1, swish), (2, up), (0, down))
    ]
    for copy in copies:
        copy.start()
    x = x_ref[...].reshape(groups * rows, width)
    copies[0].wait()
    a = jnp.dot(x, swish[...].reshape(width, hidden_count), preferred_element_type=f32)
    copies[1].wait()
    b = jnp.dot(x, up[...].reshape(width, hidden_count), preferred_element_type=f32)
    hidden = ((a / (1.0 + jnp.exp(-a))) * b).astype(bf16)
    copies[2].wait()
    out = dot_last(hidden, down[...].reshape(width, hidden_count))
    out_ref[...] = out.astype(bf16).reshape(groups, rows, width)


def finish_kernel(mixed_ref, part_ref, out_ref):
    total = mixed_ref[...].astype(f32)
    for i in range(part_ref.shape[0]):
        total = total + part_ref[i].astype(f32)
    out_ref[...] = total.astype(bf16)


def call(kernel, out_shape, scratch=(), scalars=0, flops=0, moved=0, limit=VMEM_LIMIT, left=()):
    def run(*operands):
        return pl.pallas_call(
            kernel,
            out_shape=out_shape,
            in_specs=[
                pl.BlockSpec(
                    memory_space=pltpu.SMEM if i < scalars else pl.ANY if i in left else pltpu.VMEM
                )
                for i in range(len(operands))
            ],
            scratch_shapes=list(scratch),
            compiler_params=pltpu.CompilerParams(vmem_limit_bytes=limit),
            cost_estimate=pl.CostEstimate(flops=flops, bytes_accessed=moved, transcendentals=0),
        )(*operands)

    return run


def on_device(
    lengths,
    single,
    attn_gain,
    w_query,
    w_key,
    w_value,
    w_gate,
    w_out,
    pair_rep,
    pair_gain,
    pair_proj,
    trans_gain,
    w_swish,
    w_up,
    w_down,
):
    grp_count = lax.axis_size("grp")
    pb_count = lax.axis_size("pb")
    ka_count = lax.axis_size("ka")
    ka_index = lax.axis_index("ka")
    samples, row_count, width = single.shape[1:]
    w_rows = w_query.shape[0]
    feats = width // ka_count
    hid = w_swish.shape[1]
    own_rows = samples * row_count
    chips = ka_count // 2
    held = ka_count // TP
    own = single.reshape(own_rows, width)

    line = [[i * 2 + c for i in range(pb_count * chips)] for c in range(2)]
    x = lax.all_gather(own, ("pb", "ka"), axis=0, tiled=False, axis_index_groups=line)

    early = [
        lax.dynamic_slice_in_dim(w, ka_index * feats, feats, 1)
        for w in (w_key, w_value, w_query, w_gate)
    ]
    early = jnp.concatenate(early + [w_down.T, w_swish, w_up, w_out], axis=1)
    early, pair_rep = lax.optimization_barrier((early, pair_rep))
    early = spread(early, pb_count, "pb")

    _, queries, key_blocks, key_rows, channels = pair_rep.shape
    keys_held = key_blocks * key_rows
    lanes = 2 * queries
    proj = pair_proj.reshape(channels, HEADS // 2, 2).transpose(2, 1, 0).reshape(HEADS, channels)
    bias = call(
        bias_kernel,
        (jax.ShapeDtypeStruct((keys_held, lanes), f32),) * ka_count,
        scratch=[
            pltpu.VMEM((queries * keys_held, channels), f32),
            pltpu.VMEM((ka_count, keys_held, lanes), f32),
        ],
        flops=2 * 6 * queries * keys_held * channels * HEADS,
        moved=queries * keys_held * channels * 2 + 4 * ka_count * keys_held * lanes,
    )(pair_rep.reshape(queries, keys_held, channels), pair_gain, proj)
    near = [swap(bias[i], "ka", i) for i in (1, 2, 3)]
    early, near = lax.optimization_barrier((early, near))
    early = early.reshape(pb_count * w_rows, early.shape[2])

    attn_w = jnp.broadcast_to(early[None, :, : 4 * feats], (grp_count, pb_count * w_rows, 4 * feats))
    late = early[:, 4 * feats :]
    out_w = early[:, 4 * feats + 3 * hid :]
    attn_w, late, out_w = lax.optimization_barrier((attn_w, late, out_w))
    attn_w = exchange(attn_w, "grp")

    late = [late] + [swap(late, "ka", TP)]
    out_w = [late[0][:, 3 * hid :], swap(out_w, "ka", 2), late[1][:, 3 * hid :], swap(out_w, "ka", 6)]
    late = jnp.concatenate(
        [w[:, i * hid : (i + 1) * hid] for i in range(3) for w in late] + out_w, axis=1
    )
    late = jnp.broadcast_to(late[None], (grp_count,) + late.shape)
    late, attn_w, far = lax.optimization_barrier((late, attn_w, list(bias[4:])))
    late = exchange(late, "grp")
    far = [swap(block, "ka", i + 4) for i, block in enumerate(far)]
    x, far = lax.optimization_barrier((x, far))
    other = swap(x, "ka", 1)
    bias = [bias[0]] + near + far

    line_rows = pb_count * chips * row_count
    kv_shape = (samples, line_rows, 2 * feats)
    query_shape = (chips * own_rows, 2 * feats)
    costs = dict(
        flops=2 * x.size * 3 * feats, moved=x.size * 2 + attn_w.size * 2, limit=MOST_VMEM
    )
    rows_held = [pltpu.VMEM(x.shape, bf16)] * 2 + [pltpu.SemaphoreType.DMA((pb_count,))]
    near_kv, near_query = call(
        project_kernel,
        (jax.ShapeDtypeStruct(kv_shape, bf16), jax.ShapeDtypeStruct(query_shape, f32)),
        scratch=rows_held,
        left=(0,),
        **costs,
    )(x, attn_gain, attn_w)
    gated = call(
        attention_kernel,
        jax.ShapeDtypeStruct((ka_count, own_rows, feats), bf16),
        scratch=rows_held
        + [
            pltpu.VMEM(kv_shape, bf16),
            pltpu.VMEM((ka_count, keys_held, lanes), f32),
            pltpu.VMEM((ka_count, own_rows, feats), f32),
            pltpu.VMEM((ka_count, own_rows, feats), f32),
        ],
        scalars=1,
        left=(1,),
        **costs,
    )(lengths, other, attn_gain, attn_w, near_kv, near_query, *bias)
    gated, late = lax.optimization_barrier((gated, late))
    gated = exchange(gated, "ka")
    out_w = late[:, :, held * 3 * hid :]
    other_w = swap(out_w, "ka", 1)

    rows = jax.ShapeDtypeStruct((own_rows, width), bf16)
    shared = jax.ShapeDtypeStruct((TP, own_rows, width), bf16)
    mixed, normed_t = call(
        mix_kernel,
        (rows, rows),
        scratch=[pltpu.VMEM((ka_count, own_rows, feats), f32)],
        flops=2 * own_rows * width * width,
        moved=width * width * 2,
    )(gated, out_w, other_w, own, trans_gain)

    groups = [list(range(i, i + TP)) for i in range(0, ka_count, TP)]
    normed_t = lax.all_gather(normed_t, "ka", axis=0, tiled=False, axis_index_groups=groups)
    part = call(
        transition_kernel,
        shared,
        scratch=[pltpu.VMEM((grp_count, pb_count * w_rows, held * hid), bf16)] * 3
        + [pltpu.SemaphoreType.DMA((3,))],
        left=(1,),
        flops=2 * own_rows * width * hid * ka_count * 3,
        moved=3 * width * hid * ka_count // TP * 2,
    )(normed_t, late)
    part = exchange(part, "ka", groups)
    result = call(finish_kernel, rows)(mixed, part)
    return result.reshape(1, samples, row_count, width)


def solution(mesh):
    return jax.shard_map(
        on_device,
        mesh=mesh,
        in_specs=(
            P("grp"),
            P("grp", None, ("pb", "ka"), None),
            P(),
            P(("grp", "pb"), None),
            P(("grp", "pb"), None),
            P(("grp", "pb"), None),
            P(("grp", "pb"), None),
            P(("grp", "pb"), "ka"),
            P("grp", "pb", None, "ka", None),
            P(),
            P(),
            P(),
            P(("grp", "pb"), "ka"),
            P(("grp", "pb"), "ka"),
            P("ka", ("grp", "pb")),
        ),
        out_specs=P("grp", None, ("pb", "ka"), None),
        check_vma=False,
    )
```

```python
import functools
import math

import jax
import jax.numpy as jnp
from jax import lax
from jax.experimental import pallas as pl
from jax.experimental.pallas import tpu as pltpu
from jax.sharding import PartitionSpec as P

HEADS = 16
TP = 4

epsilon = 1e-05
very_negative = -1e30
f32 = jnp.float32
bf16 = jnp.bfloat16
VMEM_LIMIT = 48 * 1024 * 1024
MOST_VMEM = 63 * 1024 * 1024


def layer_norm(inputs, scale_gain):
    mean_val = jnp.mean(inputs, axis=-1, keepdims=True)
    centred = inputs - mean_val
    spread = jnp.mean(centred * centred, axis=-1, keepdims=True)
    return centred * lax.rsqrt(spread + epsilon) * scale_gain


def dot_last(a, b, precision=None):
    return lax.dot_general(
        a, b, (((1,), (1,)), ((), ())), preferred_element_type=f32, precision=precision
    )


def exchange(blocks, axes, groups=None):
    return lax.all_to_all(
        blocks, axes, split_axis=0, concat_axis=0, tiled=True, axis_index_groups=groups
    )


def spread(block, count, axes):
    return exchange(jnp.broadcast_to(block[None], (count,) + block.shape), axes)


def gather(block, axes):
    return lax.all_gather(block, axes, axis=0, tiled=False)


def swap(block, axis, flip):
    count = lax.axis_size(axis)
    return lax.ppermute(block, axis, [(i, i ^ flip) for i in range(count)])


def bias_kernel(x_ref, gain_ref, proj_ref, *refs):
    out_refs, rows, held = refs[:-2], refs[-2], refs[-1]
    queries, keys, channels = x_ref.shape
    pairs = len(out_refs)
    normed = layer_norm(
        x_ref[...].reshape(queries * keys, channels).astype(f32), gain_ref[...].reshape(1, -1)
    )
    rows[...] = normed
    together = 256 // queries
    for start in range(0, keys, together):
        block = jnp.concatenate(
            [rows[pl.ds(start + j, queries, stride=keys), :] for j in range(together)], axis=0
        )
        bias = dot_last(proj_ref[...], block, lax.Precision.HIGHEST)
        for j in range(together):
            cols = slice(j * queries, (j + 1) * queries)
            tile = jnp.concatenate([bias[:pairs, cols], bias[pairs:, cols]], axis=1)
            held[:, start + j, :] = tile
    for flip, out_ref in enumerate(out_refs):
        out_ref[...] = held[lax.axis_index("ka") ^ flip]


def load_side(blocks, x_ref, w_ref, raw_ref, weights_ref, sems):
    chips = x_ref.shape[0] // blocks
    copies = [
        pltpu.make_async_copy(
            x_ref.at[pl.ds(b * chips, chips)], raw_ref.at[pl.ds(b * chips, chips)], sems.at[b]
        )
        for b in range(blocks)
    ]
    copies.append(pltpu.make_async_copy(w_ref, weights_ref, sems.at[blocks]))
    for copy in copies:
        copy.start()
    return copies


def project_side(samples, copies, gain_ref, raw_ref, weights_ref, held_ref, kv_ref):
    places, own_rows, width = raw_ref.shape
    feats = kv_ref.shape[2] // 2
    each = own_rows // samples
    blocks = len(copies) - 1
    chips = places // blocks
    for b in range(blocks):
        copies[b].wait()
        part = slice(b * chips, (b + 1) * chips)
        x = raw_ref[part].reshape(chips * own_rows, width).astype(f32)
        normed = layer_norm(x, gain_ref[...].reshape(1, -1)).astype(bf16)
        held_ref[part] = normed.reshape(chips, own_rows, width)
    copies[blocks].wait()
    weights = weights_ref[...].reshape(width, 4 * feats)
    normed = held_ref[...].reshape(places * own_rows, width)
    proj = jnp.dot(normed, weights[:, : 2 * feats], preferred_element_type=f32)
    proj = proj.reshape(places, samples, each, 2 * feats)
    for s in range(samples):
        kv_ref[s] = proj[:, s].reshape(places * each, 2 * feats).astype(bf16)
    rows = held_ref[pl.ds(lax.axis_index("pb") * chips, chips)].reshape(chips * own_rows, width)
    return jnp.dot(rows, weights[:, 2 * feats :], preferred_element_type=f32)


def project_kernel(x_ref, gain_ref, w_ref, kv_ref, query_ref, raw, weights, held, sems):
    blocks = lax.axis_size("pb")
    copies = load_side(blocks, x_ref, w_ref, raw, weights, sems)
    query_ref[...] = project_side(
        kv_ref.shape[0], copies, gain_ref, raw, weights, held, kv_ref
    )


def attention_kernel(length_ref, x_ref, gain_ref, w_ref, near_kv_ref, near_ref, *refs):
    count = len(refs) - 11
    bias_refs = refs[:count]
    out_ref, raw, weights, held_normed, sems, kv_ref, near, held_kv = refs[count : count + 8]
    held_bias, held_query, held_gate = refs[count + 8 :]
    blocks = lax.axis_size("pb")
    copies = load_side(blocks, x_ref, w_ref, raw, weights, sems)
    later = [
        pltpu.make_async_copy(near_ref, near, sems.at[blocks + 1]),
        pltpu.make_async_copy(near_kv_ref, kv_ref, sems.at[blocks + 2]),
    ]
    for copy in later:
        copy.start()
    places, own_rows, width = x_ref.shape
    samples, span, feats = kv_ref.shape
    feats = feats // 2
    chips = count // 2
    keys_held, lanes = bias_refs[0].shape
    q_rows = lanes // 2
    each = q_rows // count
    key_count = blocks * q_rows
    head_dim = feats // 2
    length, at = length_ref[0], lax.axis_index("ka")
    core = at % 2
    far = project_side(samples, copies, gain_ref, raw, weights, held_normed, held_kv)
    for copy in later:
        copy.wait()
    for side, proj in enumerate((near[...], far)):
        for z in range(chips):
            k = 2 * z + (core ^ side)
            part = proj[z * own_rows : (z + 1) * own_rows]
            held_query[k] = part[:, :feats]
            held_gate[k] = part[:, feats:]
    for flip in range(count):
        held_bias[at ^ flip] = bias_refs[flip][...]
    bias = jnp.concatenate(
        [
            held_bias[2 * z + (core ^ side), b * each : (b + 1) * each, :]
            for side in range(2)
            for b in range(blocks)
            for z in range(chips)
        ],
        axis=0,
    )
    index = lax.broadcasted_iota(jnp.int32, (key_count, lanes), 0)
    side = index // span
    position = ((index % span) // each) * (2 * each) + (side ^ core) * each + index % each
    live = position < length
    first = lax.broadcasted_iota(jnp.int32, (q_rows, feats), 1) < head_dim
    done = []
    for s in range(samples):
        both_sides = jnp.concatenate([kv_ref[s], held_kv[s]], axis=0)
        keys, values = both_sides[:, :feats], both_sides[:, feats:]
        rows = slice(s * each, (s + 1) * each)
        query = held_query[:, rows, :].reshape(q_rows, feats)
        both = jnp.concatenate(
            [jnp.where(first, query, 0.0), jnp.where(first, 0.0, query)], axis=0
        ).astype(bf16)
        scores = dot_last(keys, both) * (1.0 / math.sqrt(head_dim)) + bias
        scores = jnp.where(live, scores, very_negative)
        peak = jnp.max(scores, axis=0, keepdims=True)
        soft = jnp.exp(scores - peak)
        total = jnp.sum(soft, axis=0, keepdims=True)
        weighted = lax.dot_general(
            values, soft.astype(bf16), (((0,), (0,)), ((), ())), preferred_element_type=f32
        )
        attended = (weighted / total).T
        attended = jnp.where(first, attended[:q_rows], attended[q_rows:])
        gate = jax.nn.sigmoid(held_gate[:, rows, :].reshape(q_rows, feats))
        gate = gate.astype(bf16).astype(f32)
        done.append((attended * gate).reshape(count, each, feats))
        if s % 2:
            size = 2 * each
            start = s // 2 * size
            out_ref[:, start : start + size, :] = jnp.concatenate(done, axis=1).astype(bf16)
            done = []


def mix_kernel(
    gated_ref, w_ref, other_ref, single_ref, gain_ref, mixed_ref, normed_ref, held
):
    ka_count, rows, feats = gated_ref.shape
    width = single_ref.shape[1]
    chips = ka_count // 2
    at = lax.axis_index("ka")
    gated = jnp.concatenate([gated_ref[k] for k in range(ka_count)], axis=1)
    for side, ref in enumerate((w_ref, other_ref)):
        weights = ref[...].reshape(width, chips * feats)
        added = jnp.dot(gated, weights, preferred_element_type=f32)
        for flip in range(chips):
            held[at ^ (2 * flip + side)] = added[:, flip * feats : (flip + 1) * feats]
    added = jnp.concatenate([held[k] for k in range(ka_count)], axis=1)
    mixed = (single_ref[...].astype(f32) + added).astype(bf16)
    mixed_ref[...] = mixed
    normed = layer_norm(mixed.astype(f32), gain_ref[...].reshape(1, -1)).astype(bf16)
    normed_ref[...] = normed


def transition_kernel(x_ref, w_ref, out_ref, swish, up, down, sems):
    groups, rows, width = x_ref.shape
    hidden_count = down.shape[2]
    copies = [
        pltpu.make_async_copy(
            w_ref.at[:, :, pl.ds(i * hidden_count, hidden_count)], part, sems.at[i]
        )
        for i, part in ((1, swish), (2, up), (0, down))
    ]
    for copy in copies:
        copy.start()
    x = x_ref[...].reshape(groups * rows, width)
    copies[0].wait()
    a = jnp.dot(x, swish[...].reshape(width, hidden_count), preferred_element_type=f32)
    copies[1].wait()
    b = jnp.dot(x, up[...].reshape(width, hidden_count), preferred_element_type=f32)
    hidden = ((a / (1.0 + jnp.exp(-a))) * b).astype(bf16)
    copies[2].wait()
    out = dot_last(hidden, down[...].reshape(width, hidden_count))
    out_ref[...] = out.astype(bf16).reshape(groups, rows, width)


def finish_kernel(mixed_ref, part_ref, out_ref):
    total = mixed_ref[...].astype(f32)
    for i in range(part_ref.shape[0]):
        total = total + part_ref[i].astype(f32)
    out_ref[...] = total.astype(bf16)


def call(kernel, out_shape, scratch=(), scalars=0, flops=0, moved=0, limit=VMEM_LIMIT, left=()):
    def run(*operands):
        return pl.pallas_call(
            kernel,
            out_shape=out_shape,
            in_specs=[
                pl.BlockSpec(
                    memory_space=pltpu.SMEM if i < scalars else pl.ANY if i in left else pltpu.VMEM
                )
                for i in range(len(operands))
            ],
            scratch_shapes=list(scratch),
            compiler_params=pltpu.CompilerParams(vmem_limit_bytes=limit),
            cost_estimate=pl.CostEstimate(flops=flops, bytes_accessed=moved, transcendentals=0),
        )(*operands)

    return run


def on_device(
    lengths,
    single,
    attn_gain,
    w_query,
    w_key,
    w_value,
    w_gate,
    w_out,
    pair_rep,
    pair_gain,
    pair_proj,
    trans_gain,
    w_swish,
    w_up,
    w_down,
):
    grp_count = lax.axis_size("grp")
    pb_count = lax.axis_size("pb")
    ka_count = lax.axis_size("ka")
    ka_index = lax.axis_index("ka")
    samples, row_count, width = single.shape[1:]
    w_rows = w_query.shape[0]
    feats = width // ka_count
    hid = w_swish.shape[1]
    own_rows = samples * row_count
    chips = ka_count // 2
    held = ka_count // TP
    own = single.reshape(own_rows, width)

    line = [[i * 2 + c for i in range(pb_count * chips)] for c in range(2)]
    x = lax.all_gather(own, ("pb", "ka"), axis=0, tiled=False, axis_index_groups=line)

    early = [
        lax.dynamic_slice_in_dim(w, ka_index * feats, feats, 1)
        for w in (w_key, w_value, w_query, w_gate)
    ]
    early = jnp.concatenate(early + [w_down.T, w_swish, w_up, w_out], axis=1)
    early, pair_rep = lax.optimization_barrier((early, pair_rep))
    early = spread(early, pb_count, "pb")

    _, queries, key_blocks, key_rows, channels = pair_rep.shape
    keys_held = key_blocks * key_rows
    lanes = 2 * queries
    proj = pair_proj.reshape(channels, HEADS // 2, 2).transpose(2, 1, 0).reshape(HEADS, channels)
    bias = call(
        bias_kernel,
        (jax.ShapeDtypeStruct((keys_held, lanes), f32),) * ka_count,
        scratch=[
            pltpu.VMEM((queries * keys_held, channels), f32),
            pltpu.VMEM((ka_count, keys_held, lanes), f32),
        ],
        flops=2 * 6 * queries * keys_held * channels * HEADS,
        moved=queries * keys_held * channels * 2 + 4 * ka_count * keys_held * lanes,
    )(pair_rep.reshape(queries, keys_held, channels), pair_gain, proj)
    near = [swap(bias[i], "ka", i) for i in (1, 2, 3)]
    early, near = lax.optimization_barrier((early, near))
    early = early.reshape(pb_count * w_rows, early.shape[2])

    attn_w = jnp.broadcast_to(early[None, :, : 4 * feats], (grp_count, pb_count * w_rows, 4 * feats))
    late = early[:, 4 * feats :]
    out_w = early[:, 4 * feats + 3 * hid :]
    attn_w, late, out_w = lax.optimization_barrier((attn_w, late, out_w))
    attn_w = exchange(attn_w, "grp")

    late = [late] + [swap(late, "ka", TP)]
    out_w = [late[0][:, 3 * hid :], swap(out_w, "ka", 2), late[1][:, 3 * hid :], swap(out_w, "ka", 6)]
    late = jnp.concatenate(
        [w[:, i * hid : (i + 1) * hid] for i in range(3) for w in late] + out_w, axis=1
    )
    late = jnp.broadcast_to(late[None], (grp_count,) + late.shape)
    late, attn_w, far = lax.optimization_barrier((late, attn_w, list(bias[4:])))
    late = exchange(late, "grp")
    far = [swap(block, "ka", i + 4) for i, block in enumerate(far)]
    x, far = lax.optimization_barrier((x, far))
    other = swap(x, "ka", 1)
    bias = [bias[0]] + near + far

    line_rows = pb_count * chips * row_count
    kv_shape = (samples, line_rows, 2 * feats)
    query_shape = (chips * own_rows, 2 * feats)
    costs = dict(
        flops=2 * x.size * 3 * feats, moved=x.size * 2 + attn_w.size * 2, limit=MOST_VMEM
    )
    rows_held = [
        pltpu.VMEM(x.shape, bf16),
        pltpu.VMEM(attn_w.shape, bf16),
        pltpu.VMEM(x.shape, bf16),
        pltpu.SemaphoreType.DMA((pb_count + 3,)),
    ]
    near_kv, near_query = call(
        project_kernel,
        (jax.ShapeDtypeStruct(kv_shape, bf16), jax.ShapeDtypeStruct(query_shape, f32)),
        scratch=rows_held,
        left=(0, 2),
        **costs,
    )(x, attn_gain, attn_w)
    gated = call(
        attention_kernel,
        jax.ShapeDtypeStruct((ka_count, own_rows, feats), bf16),
        scratch=rows_held
        + [
            pltpu.VMEM(kv_shape, bf16),
            pltpu.VMEM(query_shape, f32),
            pltpu.VMEM(kv_shape, bf16),
            pltpu.VMEM((ka_count, keys_held, lanes), f32),
            pltpu.VMEM((ka_count, own_rows, feats), f32),
            pltpu.VMEM((ka_count, own_rows, feats), f32),
        ],
        scalars=1,
        left=(1, 3, 4, 5),
        **costs,
    )(lengths, other, attn_gain, attn_w, near_kv, near_query, *bias)
    gated, late = lax.optimization_barrier((gated, late))
    gated = exchange(gated, "ka")
    out_w = late[:, :, held * 3 * hid :]
    other_w = swap(out_w, "ka", 1)

    rows = jax.ShapeDtypeStruct((own_rows, width), bf16)
    shared = jax.ShapeDtypeStruct((TP, own_rows, width), bf16)
    mixed, normed_t = call(
        mix_kernel,
        (rows, rows),
        scratch=[pltpu.VMEM((ka_count, own_rows, feats), f32)],
        flops=2 * own_rows * width * width,
        moved=width * width * 2,
    )(gated, out_w, other_w, own, trans_gain)

    groups = [list(range(i, i + TP)) for i in range(0, ka_count, TP)]
    normed_t = lax.all_gather(normed_t, "ka", axis=0, tiled=False, axis_index_groups=groups)
    part = call(
        transition_kernel,
        shared,
        scratch=[pltpu.VMEM((grp_count, pb_count * w_rows, held * hid), bf16)] * 3
        + [pltpu.SemaphoreType.DMA((3,))],
        left=(1,),
        flops=2 * own_rows * width * hid * ka_count * 3,
        moved=3 * width * hid * ka_count // TP * 2,
    )(normed_t, late)
    part = exchange(part, "ka", groups)
    result = call(finish_kernel, rows)(mixed, part)
    return result.reshape(1, samples, row_count, width)


def solution(mesh):
    return jax.shard_map(
        on_device,
        mesh=mesh,
        in_specs=(
            P("grp"),
            P("grp", None, ("pb", "ka"), None),
            P(),
            P(("grp", "pb"), None),
            P(("grp", "pb"), None),
            P(("grp", "pb"), None),
            P(("grp", "pb"), None),
            P(("grp", "pb"), "ka"),
            P("grp", "pb", None, "ka", None),
            P(),
            P(),
            P(),
            P(("grp", "pb"), "ka"),
            P(("grp", "pb"), "ka"),
            P("ka", ("grp", "pb")),
        ),
        out_specs=P("grp", None, ("pb", "ka"), None),
        check_vma=False,
    )
```

```python
import functools
import math

import jax
import jax.numpy as jnp
from jax import lax
from jax.experimental import pallas as pl
from jax.experimental.pallas import tpu as pltpu
from jax.sharding import PartitionSpec as P

HEADS = 16
TP = 4

epsilon = 1e-05
very_negative = -1e30
f32 = jnp.float32
bf16 = jnp.bfloat16
VMEM_LIMIT = 32 * 1024 * 1024
MOST_VMEM = 32 * 1024 * 1024


def layer_norm(inputs, scale_gain):
    mean_val = jnp.mean(inputs, axis=-1, keepdims=True)
    centred = inputs - mean_val
    spread = jnp.mean(centred * centred, axis=-1, keepdims=True)
    return centred * lax.rsqrt(spread + epsilon) * scale_gain


def dot_last(a, b, precision=None):
    return lax.dot_general(
        a, b, (((1,), (1,)), ((), ())), preferred_element_type=f32, precision=precision
    )


def exchange(blocks, axes, groups=None):
    return lax.all_to_all(
        blocks, axes, split_axis=0, concat_axis=0, tiled=True, axis_index_groups=groups
    )


def spread(block, count, axes):
    return exchange(jnp.broadcast_to(block[None], (count,) + block.shape), axes)


def gather(block, axes):
    return lax.all_gather(block, axes, axis=0, tiled=False)


def swap(block, axis, flip):
    count = lax.axis_size(axis)
    return lax.ppermute(block, axis, [(i, i ^ flip) for i in range(count)])


def bias_kernel(x_ref, gain_ref, proj_ref, *refs):
    out_refs, rows, held = refs[:-2], refs[-2], refs[-1]
    queries, keys, channels = x_ref.shape
    pairs = len(out_refs)
    normed = layer_norm(
        x_ref[...].reshape(queries * keys, channels).astype(f32), gain_ref[...].reshape(1, -1)
    )
    rows[...] = normed
    together = 256 // queries
    for start in range(0, keys, together):
        block = jnp.concatenate(
            [rows[pl.ds(start + j, queries, stride=keys), :] for j in range(together)], axis=0
        )
        bias = dot_last(proj_ref[...], block, lax.Precision.HIGHEST)
        for j in range(together):
            cols = slice(j * queries, (j + 1) * queries)
            tile = jnp.concatenate([bias[:pairs, cols], bias[pairs:, cols]], axis=1)
            held[:, start + j, :] = tile
    for flip, out_ref in enumerate(out_refs):
        out_ref[...] = held[lax.axis_index("ka") ^ flip]


def place_kernel(*refs):
    for flip, ref in enumerate(refs[:-1]):
        refs[-1][lax.axis_index("ka") ^ flip] = ref[...]


def project_side(samples, x_ref, gain_ref, w_ref, held_ref, kv_ref):
    places, own_rows, width = x_ref.shape
    feats = kv_ref.shape[2] // 2
    each = own_rows // samples
    chips = places // lax.axis_size("pb")
    weights = w_ref[...].reshape(width, 4 * feats)
    x = x_ref[...].reshape(places * own_rows, width).astype(f32)
    normed = layer_norm(x, gain_ref[...].reshape(1, -1)).astype(bf16)
    held_ref[...] = normed.reshape(places, own_rows, width)
    proj = jnp.dot(normed, weights[:, : 2 * feats], preferred_element_type=f32)
    proj = proj.reshape(places, samples, each, 2 * feats)
    for s in range(samples):
        kv_ref[s] = proj[:, s].reshape(places * each, 2 * feats).astype(bf16)
    rows = held_ref[pl.ds(lax.axis_index("pb") * chips, chips)].reshape(chips * own_rows, width)
    return jnp.dot(rows, weights[:, 2 * feats :], preferred_element_type=f32)


def project_kernel(x_ref, gain_ref, w_ref, kv_ref, query_ref, held_ref):
    samples = kv_ref.shape[0]
    query_ref[...] = project_side(samples, x_ref, gain_ref, w_ref, held_ref, kv_ref)


def attention_kernel(length_ref, x_ref, gain_ref, w_ref, kv_ref, near_ref, bias_ref, *refs):
    out_ref, held_normed, held_kv, held_query, held_gate = refs
    count, keys_held, lanes = bias_ref.shape
    places, own_rows, width = x_ref.shape
    samples, span, feats = kv_ref.shape
    feats = feats // 2
    chips = count // 2
    blocks = places // chips
    q_rows = lanes // 2
    each = q_rows // count
    key_count = blocks * q_rows
    head_dim = feats // 2
    length, at = length_ref[0], lax.axis_index("ka")
    core = at % 2
    far = project_side(samples, x_ref, gain_ref, w_ref, held_normed, held_kv)
    for side, proj in enumerate((near_ref[...], far)):
        for z in range(chips):
            k = 2 * z + (core ^ side)
            part = proj[z * own_rows : (z + 1) * own_rows]
            held_query[k] = part[:, :feats]
            held_gate[k] = part[:, feats:]
    bias = jnp.concatenate(
        [
            bias_ref[2 * z + (core ^ side), b * each : (b + 1) * each, :]
            for side in range(2)
            for b in range(blocks)
            for z in range(chips)
        ],
        axis=0,
    )
    index = lax.broadcasted_iota(jnp.int32, (key_count, lanes), 0)
    side = index // span
    position = ((index % span) // each) * (2 * each) + (side ^ core) * each + index % each
    live = position < length
    first = lax.broadcasted_iota(jnp.int32, (q_rows, feats), 1) < head_dim
    done = []
    for s in range(samples):
        both_sides = jnp.concatenate([kv_ref[s], held_kv[s]], axis=0)
        keys, values = both_sides[:, :feats], both_sides[:, feats:]
        rows = slice(s * each, (s + 1) * each)
        query = held_query[:, rows, :].reshape(q_rows, feats)
        both = jnp.concatenate(
            [jnp.where(first, query, 0.0), jnp.where(first, 0.0, query)], axis=0
        ).astype(bf16)
        scores = dot_last(keys, both) * (1.0 / math.sqrt(head_dim)) + bias
        scores = jnp.where(live, scores, very_negative)
        peak = jnp.max(scores, axis=0, keepdims=True)
        soft = jnp.exp(scores - peak)
        total = jnp.sum(soft, axis=0, keepdims=True)
        weighted = lax.dot_general(
            values, soft.astype(bf16), (((0,), (0,)), ((), ())), preferred_element_type=f32
        )
        attended = (weighted / total).T
        attended = jnp.where(first, attended[:q_rows], attended[q_rows:])
        gate = jax.nn.sigmoid(held_gate[:, rows, :].reshape(q_rows, feats))
        gate = gate.astype(bf16).astype(f32)
        done.append((attended * gate).reshape(count, each, feats))
        if s % 2:
            size = 2 * each
            start = s // 2 * size
            out_ref[:, start : start + size, :] = jnp.concatenate(done, axis=1).astype(bf16)
            done = []


def mix_kernel(
    gated_ref, w_ref, other_ref, single_ref, gain_ref, mixed_ref, normed_ref, held
):
    ka_count, rows, feats = gated_ref.shape
    width = single_ref.shape[1]
    chips = ka_count // 2
    at = lax.axis_index("ka")
    gated = jnp.concatenate([gated_ref[k] for k in range(ka_count)], axis=1)
    for side, ref in enumerate((w_ref, other_ref)):
        weights = ref[...].reshape(width, chips * feats)
        added = jnp.dot(gated, weights, preferred_element_type=f32)
        for flip in range(chips):
            held[at ^ (2 * flip + side)] = added[:, flip * feats : (flip + 1) * feats]
    added = jnp.concatenate([held[k] for k in range(ka_count)], axis=1)
    mixed = (single_ref[...].astype(f32) + added).astype(bf16)
    mixed_ref[...] = mixed
    normed = layer_norm(mixed.astype(f32), gain_ref[...].reshape(1, -1)).astype(bf16)
    normed_ref[...] = normed


def transition_kernel(x_ref, w_ref, out_ref):
    groups, rows, width = x_ref.shape
    part = w_ref.shape[2] // 4
    x = x_ref[...].reshape(groups * rows, width)
    down, swish, up = (
        w_ref[:, :, i * part : (i + 1) * part].reshape(width, part) for i in range(3)
    )
    a = jnp.dot(x, swish, preferred_element_type=f32)
    b = jnp.dot(x, up, preferred_element_type=f32)
    hidden = ((a / (1.0 + jnp.exp(-a))) * b).astype(bf16)
    out_ref[...] = dot_last(hidden, down).astype(bf16).reshape(groups, rows, width)


def finish_kernel(mixed_ref, part_ref, out_ref):
    total = mixed_ref[...].astype(f32)
    for i in range(part_ref.shape[0]):
        total = total + part_ref[i].astype(f32)
    out_ref[...] = total.astype(bf16)


def call(kernel, out_shape, scratch=(), scalars=0, flops=0, moved=0, limit=VMEM_LIMIT, left=()):
    def run(*operands):
        return pl.pallas_call(
            kernel,
            out_shape=out_shape,
            in_specs=[
                pl.BlockSpec(
                    memory_space=pltpu.SMEM if i < scalars else pl.ANY if i in left else pltpu.VMEM
                )
                for i in range(len(operands))
            ],
            scratch_shapes=list(scratch),
            compiler_params=pltpu.CompilerParams(vmem_limit_bytes=limit),
            cost_estimate=pl.CostEstimate(flops=flops, bytes_accessed=moved, transcendentals=0),
        )(*operands)

    return run


def on_device(
    lengths,
    single,
    attn_gain,
    w_query,
    w_key,
    w_value,
    w_gate,
    w_out,
    pair_rep,
    pair_gain,
    pair_proj,
    trans_gain,
    w_swish,
    w_up,
    w_down,
):
    grp_count = lax.axis_size("grp")
    pb_count = lax.axis_size("pb")
    ka_count = lax.axis_size("ka")
    ka_index = lax.axis_index("ka")
    samples, row_count, width = single.shape[1:]
    w_rows = w_query.shape[0]
    feats = width // ka_count
    hid = w_swish.shape[1]
    own_rows = samples * row_count
    chips = ka_count // 2
    held = ka_count // TP
    own = single.reshape(own_rows, width)

    line = [[i * 2 + c for i in range(pb_count * chips)] for c in range(2)]
    x = lax.all_gather(own, ("pb", "ka"), axis=0, tiled=False, axis_index_groups=line)

    early = [
        lax.dynamic_slice_in_dim(w, ka_index * feats, feats, 1)
        for w in (w_key, w_value, w_query, w_gate)
    ]
    early = jnp.concatenate(early + [w_down.T, w_swish, w_up, w_out], axis=1)
    early, pair_rep = lax.optimization_barrier((early, pair_rep))
    early = spread(early, pb_count, "pb")

    _, queries, key_blocks, key_rows, channels = pair_rep.shape
    keys_held = key_blocks * key_rows
    lanes = 2 * queries
    proj = pair_proj.reshape(channels, HEADS // 2, 2).transpose(2, 1, 0).reshape(HEADS, channels)
    bias = call(
        bias_kernel,
        (jax.ShapeDtypeStruct((keys_held, lanes), f32),) * ka_count,
        scratch=[
            pltpu.VMEM((queries * keys_held, channels), f32),
            pltpu.VMEM((ka_count, keys_held, lanes), f32),
        ],
        flops=2 * 6 * queries * keys_held * channels * HEADS,
        moved=queries * keys_held * channels * 2 + 4 * ka_count * keys_held * lanes,
    )(pair_rep.reshape(queries, keys_held, channels), pair_gain, proj)
    near = [swap(bias[i], "ka", i) for i in (1, 2, 3)]
    early, near = lax.optimization_barrier((early, near))
    early = early.reshape(pb_count * w_rows, early.shape[2])

    attn_w = jnp.broadcast_to(early[None, :, : 4 * feats], (grp_count, pb_count * w_rows, 4 * feats))
    late = early[:, 4 * feats :]
    out_w = early[:, 4 * feats + 3 * hid :]
    attn_w, late, out_w = lax.optimization_barrier((attn_w, late, out_w))
    attn_w = exchange(attn_w, "grp")

    late = [late] + [swap(late, "ka", TP)]
    out_w = [late[0][:, 3 * hid :], swap(out_w, "ka", 2), late[1][:, 3 * hid :], swap(out_w, "ka", 6)]
    late = jnp.concatenate(
        [w[:, i * hid : (i + 1) * hid] for i in range(3) for w in late] + out_w, axis=1
    )
    late = jnp.broadcast_to(late[None], (grp_count,) + late.shape)
    late, attn_w, far = lax.optimization_barrier((late, attn_w, list(bias[4:])))
    late = exchange(late, "grp")
    far = [swap(block, "ka", i + 4) for i, block in enumerate(far)]
    bias = call(
        place_kernel, jax.ShapeDtypeStruct((ka_count, keys_held, lanes), f32)
    )(bias[0], *near, *far)
    x, bias = lax.optimization_barrier((x, bias))
    other = swap(x, "ka", 1)

    line_rows = pb_count * chips * row_count
    kv_shape = (samples, line_rows, 2 * feats)
    query_shape = (chips * own_rows, 2 * feats)
    costs = dict(
        flops=2 * x.size * 3 * feats, moved=x.size * 2 + attn_w.size * 2, limit=MOST_VMEM
    )
    near_kv, near_query = call(
        project_kernel,
        (jax.ShapeDtypeStruct(kv_shape, bf16), jax.ShapeDtypeStruct(query_shape, f32)),
        scratch=[pltpu.VMEM(x.shape, bf16)],
        **costs,
    )(x, attn_gain, attn_w)
    gated = call(
        attention_kernel,
        jax.ShapeDtypeStruct((ka_count, own_rows, feats), bf16),
        scratch=[
            pltpu.VMEM(x.shape, bf16),
            pltpu.VMEM(kv_shape, bf16),
            pltpu.VMEM((ka_count, own_rows, feats), f32),
            pltpu.VMEM((ka_count, own_rows, feats), f32),
        ],
        scalars=1,
        **costs,
    )(lengths, other, attn_gain, attn_w, near_kv, near_query, bias)
    gated, late = lax.optimization_barrier((gated, late))
    gated = exchange(gated, "ka")
    out_w = late[:, :, held * 3 * hid :]
    other_w = swap(out_w, "ka", 1)

    rows = jax.ShapeDtypeStruct((own_rows, width), bf16)
    shared = jax.ShapeDtypeStruct((TP, own_rows, width), bf16)
    mixed, normed_t = call(
        mix_kernel,
        (rows, rows),
        scratch=[pltpu.VMEM((ka_count, own_rows, feats), f32)],
        flops=2 * own_rows * width * width,
        moved=width * width * 2,
    )(gated, out_w, other_w, own, trans_gain)

    groups = [list(range(i, i + TP)) for i in range(0, ka_count, TP)]
    normed_t = lax.all_gather(normed_t, "ka", axis=0, tiled=False, axis_index_groups=groups)
    part = call(
        transition_kernel,
        shared,

        flops=2 * own_rows * width * hid * ka_count * 3,
        moved=3 * width * hid * ka_count // TP * 2,
    )(normed_t, late)
    part = exchange(part, "ka", groups)
    result = call(finish_kernel, rows)(mixed, part)
    return result.reshape(1, samples, row_count, width)


def solution(mesh):
    return jax.shard_map(
        on_device,
        mesh=mesh,
        in_specs=(
            P("grp"),
            P("grp", None, ("pb", "ka"), None),
            P(),
            P(("grp", "pb"), None),
            P(("grp", "pb"), None),
            P(("grp", "pb"), None),
            P(("grp", "pb"), None),
            P(("grp", "pb"), "ka"),
            P("grp", "pb", None, "ka", None),
            P(),
            P(),
            P(),
            P(("grp", "pb"), "ka"),
            P(("grp", "pb"), "ka"),
            P("ka", ("grp", "pb")),
        ),
        out_specs=P("grp", None, ("pb", "ka"), None),
        check_vma=False,
    )
```

```python
import functools
import math

import jax
import jax.numpy as jnp
from jax import lax
from jax.experimental import pallas as pl
from jax.experimental.pallas import tpu as pltpu
from jax.sharding import PartitionSpec as P

HEADS = 16
TP = 4

epsilon = 1e-05
very_negative = -1e30
f32 = jnp.float32
bf16 = jnp.bfloat16
VMEM_LIMIT = 32 * 1024 * 1024
MOST_VMEM = 32 * 1024 * 1024


def layer_norm(inputs, scale_gain):
    mean_val = jnp.mean(inputs, axis=-1, keepdims=True)
    centred = inputs - mean_val
    spread = jnp.mean(centred * centred, axis=-1, keepdims=True)
    return centred * lax.rsqrt(spread + epsilon) * scale_gain


def dot_last(a, b, precision=None):
    return lax.dot_general(
        a, b, (((1,), (1,)), ((), ())), preferred_element_type=f32, precision=precision
    )


def exchange(blocks, axes, groups=None):
    return lax.all_to_all(
        blocks, axes, split_axis=0, concat_axis=0, tiled=True, axis_index_groups=groups
    )


def spread(block, count, axes):
    return exchange(jnp.broadcast_to(block[None], (count,) + block.shape), axes)


def gather(block, axes):
    return lax.all_gather(block, axes, axis=0, tiled=False)


def swap(block, axis, flip):
    count = lax.axis_size(axis)
    return lax.ppermute(block, axis, [(i, i ^ flip) for i in range(count)])


def bias_kernel(x_ref, gain_ref, proj_ref, keep_ref, send_ref, rows, held):
    queries, keys, channels = x_ref.shape
    pairs = held.shape[0]
    normed = layer_norm(
        x_ref[...].reshape(queries * keys, channels).astype(f32), gain_ref[...].reshape(1, -1)
    )
    rows[...] = normed
    together = 256 // queries
    for start in range(0, keys, together):
        block = jnp.concatenate(
            [rows[pl.ds(start + j, queries, stride=keys), :] for j in range(together)], axis=0
        )
        bias = dot_last(proj_ref[...], block, lax.Precision.HIGHEST)
        for j in range(together):
            cols = slice(j * queries, (j + 1) * queries)
            tile = jnp.concatenate([bias[:pairs, cols], bias[pairs:, cols]], axis=1)
            held[:, start + j, :] = tile
    for i in range(pairs // 2):
        keep_ref[i] = held[lax.axis_index("ka") ^ (2 * i)]
        send_ref[i] = held[lax.axis_index("ka") ^ (2 * i + 1)]


def second_kernel(keep_ref, one_ref, out_ref):
    for i in range(2):
        out_ref[2 * i] = keep_ref[2 * i + 1]
        out_ref[2 * i + 1] = one_ref[2 * i + 1]


def third_kernel(keep_ref, one_ref, two_ref, out_ref):
    out_ref[0] = keep_ref[2]
    out_ref[1] = one_ref[2]
    out_ref[2] = two_ref[2]
    out_ref[3] = two_ref[3]


def place_kernel(keep_ref, one_ref, two_ref, four_ref, out_ref):
    at = lax.axis_index("ka")
    out_ref[at] = keep_ref[0]
    out_ref[at ^ 1] = one_ref[0]
    out_ref[at ^ 2] = two_ref[0]
    out_ref[at ^ 3] = two_ref[1]
    for i in range(four_ref.shape[0]):
        out_ref[at ^ (4 + i)] = four_ref[i]


def project_side(samples, x_ref, gain_ref, w_ref, held_ref, kv_ref):
    places, own_rows, width = x_ref.shape
    feats = kv_ref.shape[2] // 2
    each = own_rows // samples
    chips = places // lax.axis_size("pb")
    weights = w_ref[:, :, : 4 * feats].reshape(width, 4 * feats)
    x = x_ref[...].reshape(places * own_rows, width).astype(f32)
    normed = layer_norm(x, gain_ref[...].reshape(1, -1)).astype(bf16)
    held_ref[...] = normed.reshape(places, own_rows, width)
    proj = jnp.dot(normed, weights[:, : 2 * feats], preferred_element_type=f32)
    proj = proj.reshape(places, samples, each, 2 * feats)
    for s in range(samples):
        kv_ref[s] = proj[:, s].reshape(places * each, 2 * feats).astype(bf16)
    rows = held_ref[pl.ds(lax.axis_index("pb") * chips, chips)].reshape(chips * own_rows, width)
    return jnp.dot(rows, weights[:, 2 * feats :], preferred_element_type=f32)


def project_kernel(x_ref, gain_ref, w_ref, kv_ref, query_ref, held_ref):
    samples = kv_ref.shape[0]
    query_ref[...] = project_side(samples, x_ref, gain_ref, w_ref, held_ref, kv_ref)


def attention_kernel(length_ref, x_ref, gain_ref, w_ref, kv_ref, near_ref, bias_ref, *refs):
    out_ref, held_normed, held_kv, held_query, held_gate = refs
    count, keys_held, lanes = bias_ref.shape
    places, own_rows, width = x_ref.shape
    samples, span, feats = kv_ref.shape
    feats = feats // 2
    chips = count // 2
    blocks = places // chips
    q_rows = lanes // 2
    each = q_rows // count
    key_count = blocks * q_rows
    head_dim = feats // 2
    length, at = length_ref[0], lax.axis_index("ka")
    core = at % 2
    far = project_side(samples, x_ref, gain_ref, w_ref, held_normed, held_kv)
    for side, proj in enumerate((near_ref[...], far)):
        for z in range(chips):
            k = 2 * z + (core ^ side)
            part = proj[z * own_rows : (z + 1) * own_rows]
            held_query[k] = part[:, :feats]
            held_gate[k] = part[:, feats:]
    bias = jnp.concatenate(
        [
            bias_ref[2 * z + (core ^ side), b * each : (b + 1) * each, :]
            for side in range(2)
            for b in range(blocks)
            for z in range(chips)
        ],
        axis=0,
    )
    index = lax.broadcasted_iota(jnp.int32, (key_count, lanes), 0)
    side = index // span
    position = ((index % span) // each) * (2 * each) + (side ^ core) * each + index % each
    live = position < length
    first = lax.broadcasted_iota(jnp.int32, (q_rows, feats), 1) < head_dim
    done = []
    for s in range(samples):
        both_sides = jnp.concatenate([kv_ref[s], held_kv[s]], axis=0)
        keys, values = both_sides[:, :feats], both_sides[:, feats:]
        rows = slice(s * each, (s + 1) * each)
        query = held_query[:, rows, :].reshape(q_rows, feats)
        both = jnp.concatenate(
            [jnp.where(first, query, 0.0), jnp.where(first, 0.0, query)], axis=0
        ).astype(bf16)
        scores = dot_last(keys, both) * (1.0 / math.sqrt(head_dim)) + bias
        scores = jnp.where(live, scores, very_negative)
        peak = jnp.max(scores, axis=0, keepdims=True)
        soft = jnp.exp(scores - peak)
        total = jnp.sum(soft, axis=0, keepdims=True)
        weighted = lax.dot_general(
            values, soft.astype(bf16), (((0,), (0,)), ((), ())), preferred_element_type=f32
        )
        attended = (weighted / total).T
        attended = jnp.where(first, attended[:q_rows], attended[q_rows:])
        gate = jax.nn.sigmoid(held_gate[:, rows, :].reshape(q_rows, feats))
        gate = gate.astype(bf16).astype(f32)
        done.append((attended * gate).reshape(count, each, feats))
        if s % 2:
            size = 2 * each
            start = s // 2 * size
            out_ref[:, start : start + size, :] = jnp.concatenate(done, axis=1).astype(bf16)
            done = []


def mix_kernel(
    gated_ref, w_ref, other_ref, single_ref, gain_ref, mixed_ref, normed_ref, held
):
    ka_count, rows, feats = gated_ref.shape
    width = single_ref.shape[1]
    chips = ka_count // 2
    at = lax.axis_index("ka")
    gated = jnp.concatenate([gated_ref[k] for k in range(ka_count)], axis=1)
    for side, ref in enumerate((w_ref, other_ref)):
        weights = ref[...].reshape(width, chips * feats)
        added = jnp.dot(gated, weights, preferred_element_type=f32)
        for i, flip in enumerate((0, 4, 2, 6)):
            held[at ^ (flip + side)] = added[:, i * feats : (i + 1) * feats]
    added = jnp.concatenate([held[k] for k in range(ka_count)], axis=1)
    mixed = (single_ref[...].astype(f32) + added).astype(bf16)
    mixed_ref[...] = mixed
    normed = layer_norm(mixed.astype(f32), gain_ref[...].reshape(1, -1)).astype(bf16)
    normed_ref[...] = normed


def transition_kernel(x_ref, w_ref, out_ref):
    groups, rows, width = x_ref.shape
    part = w_ref.shape[2] // 3
    x = x_ref[...].reshape(groups * rows, width)
    down, swish, up = (
        w_ref[:, :, i * part : (i + 1) * part].reshape(width, part) for i in range(3)
    )
    a = jnp.dot(x, swish, preferred_element_type=f32)
    b = jnp.dot(x, up, preferred_element_type=f32)
    hidden = ((a / (1.0 + jnp.exp(-a))) * b).astype(bf16)
    out_ref[...] = dot_last(hidden, down).astype(bf16).reshape(groups, rows, width)


def finish_kernel(mixed_ref, part_ref, out_ref):
    total = mixed_ref[...].astype(f32)
    for i in range(part_ref.shape[0]):
        total = total + part_ref[i].astype(f32)
    out_ref[...] = total.astype(bf16)


def call(kernel, out_shape, scratch=(), scalars=0, flops=0, moved=0, limit=VMEM_LIMIT, left=()):
    def run(*operands):
        return pl.pallas_call(
            kernel,
            out_shape=out_shape,
            in_specs=[
                pl.BlockSpec(
                    memory_space=pltpu.SMEM if i < scalars else pl.ANY if i in left else pltpu.VMEM
                )
                for i in range(len(operands))
            ],
            scratch_shapes=list(scratch),
            compiler_params=pltpu.CompilerParams(vmem_limit_bytes=limit),
            cost_estimate=pl.CostEstimate(flops=flops, bytes_accessed=moved, transcendentals=0),
        )(*operands)

    return run


def on_device(
    lengths,
    single,
    attn_gain,
    w_query,
    w_key,
    w_value,
    w_gate,
    w_out,
    pair_rep,
    pair_gain,
    pair_proj,
    trans_gain,
    w_swish,
    w_up,
    w_down,
):
    grp_count = lax.axis_size("grp")
    pb_count = lax.axis_size("pb")
    ka_count = lax.axis_size("ka")
    ka_index = lax.axis_index("ka")
    samples, row_count, width = single.shape[1:]
    w_rows = w_query.shape[0]
    feats = width // ka_count
    hid = w_swish.shape[1]
    own_rows = samples * row_count
    chips = ka_count // 2
    held = ka_count // TP
    own = single.reshape(own_rows, width)

    line = [[i * 2 + c for i in range(pb_count * chips)] for c in range(2)]
    x = lax.all_gather(own, ("pb", "ka"), axis=0, tiled=False, axis_index_groups=line)

    early = [
        lax.dynamic_slice_in_dim(w, ka_index * feats, feats, 1)
        for w in (w_key, w_value, w_query, w_gate)
    ]
    early = jnp.concatenate(early + [w_out, w_down.T, w_swish, w_up], axis=1)
    early, pair_rep = lax.optimization_barrier((early, pair_rep))
    early = spread(early, pb_count, "pb")

    _, queries, key_blocks, key_rows, channels = pair_rep.shape
    keys_held = key_blocks * key_rows
    lanes = 2 * queries
    proj = pair_proj.reshape(channels, HEADS // 2, 2).transpose(2, 1, 0).reshape(HEADS, channels)
    half = jax.ShapeDtypeStruct((ka_count // 2, keys_held, lanes), f32)
    keep, one = call(
        bias_kernel,
        (half, half),
        scratch=[
            pltpu.VMEM((queries * keys_held, channels), f32),
            pltpu.VMEM((ka_count, keys_held, lanes), f32),
        ],
        flops=2 * 6 * queries * keys_held * channels * HEADS,
        moved=queries * keys_held * channels * 2 + 4 * ka_count * keys_held * lanes,
    )(pair_rep.reshape(queries, keys_held, channels), pair_gain, proj)
    one = swap(one, "ka", 1)
    two = swap(call(second_kernel, half)(keep, one), "ka", 2)
    early, two = lax.optimization_barrier((early, two))
    early = early.reshape(pb_count * w_rows, early.shape[2])

    split = 5 * feats
    attn_w = jnp.broadcast_to(early[None, :, :split], (grp_count, pb_count * w_rows, split))
    late = early[:, split:]
    attn_w, late = lax.optimization_barrier((attn_w, late))
    attn_w = exchange(attn_w, "grp")

    late = [late, swap(late, "ka", TP)]
    late = jnp.concatenate([w[:, i * hid : (i + 1) * hid] for i in range(3) for w in late], axis=1)
    late = jnp.broadcast_to(late[None], (grp_count,) + late.shape)
    late, attn_w, two = lax.optimization_barrier((late, attn_w, two))
    late = exchange(late, "grp")
    four = swap(call(third_kernel, half)(keep, one, two), "ka", 4)
    bias = call(
        place_kernel, jax.ShapeDtypeStruct((ka_count, keys_held, lanes), f32)
    )(keep, one, two, four)

    out_w = attn_w[:, :, 4 * feats :]
    for flip in (4, 2):
        out_w = jnp.concatenate([out_w, swap(out_w, "ka", flip)], axis=2)
    x, bias, out_w = lax.optimization_barrier((x, bias, out_w))
    other = swap(x, "ka", 1)
    other_w = swap(out_w, "ka", 1)
    attn_w, late = lax.optimization_barrier((attn_w, late))

    line_rows = pb_count * chips * row_count
    kv_shape = (samples, line_rows, 2 * feats)
    query_shape = (chips * own_rows, 2 * feats)
    costs = dict(
        flops=2 * x.size * 3 * feats, moved=x.size * 2 + attn_w.size * 2, limit=MOST_VMEM
    )
    near_kv, near_query = call(
        project_kernel,
        (jax.ShapeDtypeStruct(kv_shape, bf16), jax.ShapeDtypeStruct(query_shape, f32)),
        scratch=[pltpu.VMEM(x.shape, bf16)],
        **costs,
    )(x, attn_gain, attn_w)
    gated = call(
        attention_kernel,
        jax.ShapeDtypeStruct((ka_count, own_rows, feats), bf16),
        scratch=[
            pltpu.VMEM(x.shape, bf16),
            pltpu.VMEM(kv_shape, bf16),
            pltpu.VMEM((ka_count, own_rows, feats), f32),
            pltpu.VMEM((ka_count, own_rows, feats), f32),
        ],
        scalars=1,
        **costs,
    )(lengths, other, attn_gain, attn_w, near_kv, near_query, bias)
    gated = exchange(gated, "ka")

    rows = jax.ShapeDtypeStruct((own_rows, width), bf16)
    shared = jax.ShapeDtypeStruct((TP, own_rows, width), bf16)
    mixed, normed_t = call(
        mix_kernel,
        (rows, rows),
        scratch=[pltpu.VMEM((ka_count, own_rows, feats), f32)],
        flops=2 * own_rows * width * width,
        moved=width * width * 2,
    )(gated, out_w, other_w, own, trans_gain)

    groups = [list(range(i, i + TP)) for i in range(0, ka_count, TP)]
    normed_t = lax.all_gather(normed_t, "ka", axis=0, tiled=False, axis_index_groups=groups)
    part = call(
        transition_kernel,
        shared,

        flops=2 * own_rows * width * hid * ka_count * 3,
        moved=3 * width * hid * ka_count // TP * 2,
    )(normed_t, late)
    part = exchange(part, "ka", groups)
    result = call(finish_kernel, rows)(mixed, part)
    return result.reshape(1, samples, row_count, width)


def solution(mesh):
    return jax.shard_map(
        on_device,
        mesh=mesh,
        in_specs=(
            P("grp"),
            P("grp", None, ("pb", "ka"), None),
            P(),
            P(("grp", "pb"), None),
            P(("grp", "pb"), None),
            P(("grp", "pb"), None),
            P(("grp", "pb"), None),
            P(("grp", "pb"), "ka"),
            P("grp", "pb", None, "ka", None),
            P(),
            P(),
            P(),
            P(("grp", "pb"), "ka"),
            P(("grp", "pb"), "ka"),
            P("ka", ("grp", "pb")),
        ),
        out_specs=P("grp", None, ("pb", "ka"), None),
        check_vma=False,
    )
```

```python
import functools
import math

import jax
import jax.numpy as jnp
from jax import lax
from jax.experimental import pallas as pl
from jax.experimental.pallas import tpu as pltpu
from jax.sharding import PartitionSpec as P

HEADS = 16
TP = 4

epsilon = 1e-05
very_negative = -1e30
f32 = jnp.float32
bf16 = jnp.bfloat16
VMEM_LIMIT = 32 * 1024 * 1024
MOST_VMEM = 32 * 1024 * 1024


def layer_norm(inputs, scale_gain):
    mean_val = jnp.mean(inputs, axis=-1, keepdims=True)
    centred = inputs - mean_val
    spread = jnp.mean(centred * centred, axis=-1, keepdims=True)
    return centred * lax.rsqrt(spread + epsilon) * scale_gain


def dot_last(a, b, precision=None):
    return lax.dot_general(
        a, b, (((1,), (1,)), ((), ())), preferred_element_type=f32, precision=precision
    )


def exchange(blocks, axes, groups=None):
    return lax.all_to_all(
        blocks, axes, split_axis=0, concat_axis=0, tiled=True, axis_index_groups=groups
    )


def spread(block, count, axes):
    return exchange(jnp.broadcast_to(block[None], (count,) + block.shape), axes)


def gather(block, axes):
    return lax.all_gather(block, axes, axis=0, tiled=False)


def swap(block, axis, flip):
    count = lax.axis_size(axis)
    return lax.ppermute(block, axis, [(i, i ^ flip) for i in range(count)])


def bias_kernel(x_ref, gain_ref, proj_ref, keep_ref, send_ref, rows, held):
    queries, keys, channels = x_ref.shape
    pairs = held.shape[0]
    normed = layer_norm(
        x_ref[...].reshape(queries * keys, channels).astype(f32), gain_ref[...].reshape(1, -1)
    )
    rows[...] = normed
    together = 256 // queries
    for start in range(0, keys, together):
        block = jnp.concatenate(
            [rows[pl.ds(start + j, queries, stride=keys), :] for j in range(together)], axis=0
        )
        bias = dot_last(proj_ref[...], block, lax.Precision.HIGHEST)
        for j in range(together):
            cols = slice(j * queries, (j + 1) * queries)
            tile = jnp.concatenate([bias[:pairs, cols], bias[pairs:, cols]], axis=1)
            held[:, start + j, :] = tile
    for i in range(pairs // 2):
        keep_ref[i] = held[lax.axis_index("ka") ^ (2 * i)]
        send_ref[i] = held[lax.axis_index("ka") ^ (2 * i + 1)]


def second_kernel(keep_ref, one_ref, out_ref):
    for i in range(2):
        out_ref[2 * i] = keep_ref[2 * i + 1]
        out_ref[2 * i + 1] = one_ref[2 * i + 1]


def third_kernel(keep_ref, one_ref, two_ref, out_ref):
    out_ref[0] = keep_ref[2]
    out_ref[1] = one_ref[2]
    out_ref[2] = two_ref[2]
    out_ref[3] = two_ref[3]


def place_kernel(keep_ref, one_ref, two_ref, four_ref, out_ref):
    at = lax.axis_index("ka")
    out_ref[at] = keep_ref[0]
    out_ref[at ^ 1] = one_ref[0]
    out_ref[at ^ 2] = two_ref[0]
    out_ref[at ^ 3] = two_ref[1]
    for i in range(four_ref.shape[0]):
        out_ref[at ^ (4 + i)] = four_ref[i]


def project_side(samples, x_ref, gain_ref, w_ref, held_ref, kv_ref):
    places, own_rows, width = x_ref.shape
    feats = kv_ref.shape[2] // 2
    each = own_rows // samples
    chips = places // lax.axis_size("pb")
    weights = w_ref[...].reshape(width, 4 * feats)
    x = x_ref[...].reshape(places * own_rows, width).astype(f32)
    normed = layer_norm(x, gain_ref[...].reshape(1, -1)).astype(bf16)
    held_ref[...] = normed.reshape(places, own_rows, width)
    proj = jnp.dot(normed, weights[:, : 2 * feats], preferred_element_type=f32)
    proj = proj.reshape(places, samples, each, 2 * feats)
    for s in range(samples):
        kv_ref[s] = proj[:, s].reshape(places * each, 2 * feats).astype(bf16)
    rows = held_ref[pl.ds(lax.axis_index("pb") * chips, chips)].reshape(chips * own_rows, width)
    return jnp.dot(rows, weights[:, 2 * feats :], preferred_element_type=f32)


def project_kernel(x_ref, gain_ref, w_ref, kv_ref, query_ref, held_ref):
    samples = kv_ref.shape[0]
    query_ref[...] = project_side(samples, x_ref, gain_ref, w_ref, held_ref, kv_ref)


def attention_kernel(length_ref, x_ref, gain_ref, w_ref, kv_ref, near_ref, bias_ref, *refs):
    out_ref, held_normed, held_kv, held_query, held_gate = refs
    count, keys_held, lanes = bias_ref.shape
    places, own_rows, width = x_ref.shape
    samples, span, feats = kv_ref.shape
    feats = feats // 2
    chips = count // 2
    blocks = places // chips
    q_rows = lanes // 2
    each = q_rows // count
    key_count = blocks * q_rows
    head_dim = feats // 2
    length, at = length_ref[0], lax.axis_index("ka")
    core = at % 2
    far = project_side(samples, x_ref, gain_ref, w_ref, held_normed, held_kv)
    for side, proj in enumerate((near_ref[...], far)):
        for z in range(chips):
            k = 2 * z + (core ^ side)
            part = proj[z * own_rows : (z + 1) * own_rows]
            held_query[k] = part[:, :feats]
            held_gate[k] = part[:, feats:]
    bias = jnp.concatenate(
        [
            bias_ref[2 * z + (core ^ side), b * each : (b + 1) * each, :]
            for side in range(2)
            for b in range(blocks)
            for z in range(chips)
        ],
        axis=0,
    )
    index = lax.broadcasted_iota(jnp.int32, (key_count, lanes), 0)
    side = index // span
    position = ((index % span) // each) * (2 * each) + (side ^ core) * each + index % each
    live = position < length
    first = lax.broadcasted_iota(jnp.int32, (q_rows, feats), 1) < head_dim
    done = []
    for s in range(samples):
        both_sides = jnp.concatenate([kv_ref[s], held_kv[s]], axis=0)
        keys, values = both_sides[:, :feats], both_sides[:, feats:]
        rows = slice(s * each, (s + 1) * each)
        query = held_query[:, rows, :].reshape(q_rows, feats)
        both = jnp.concatenate(
            [jnp.where(first, query, 0.0), jnp.where(first, 0.0, query)], axis=0
        ).astype(bf16)
        scores = dot_last(keys, both) * (1.0 / math.sqrt(head_dim)) + bias
        scores = jnp.where(live, scores, very_negative)
        peak = jnp.max(scores, axis=0, keepdims=True)
        soft = jnp.exp(scores - peak)
        total = jnp.sum(soft, axis=0, keepdims=True)
        weighted = lax.dot_general(
            values, soft.astype(bf16), (((0,), (0,)), ((), ())), preferred_element_type=f32
        )
        attended = (weighted / total).T
        attended = jnp.where(first, attended[:q_rows], attended[q_rows:])
        gate = jax.nn.sigmoid(held_gate[:, rows, :].reshape(q_rows, feats))
        gate = gate.astype(bf16).astype(f32)
        done.append((attended * gate).reshape(count, each, feats))
        if s % 2:
            size = 2 * each
            start = s // 2 * size
            out_ref[:, start : start + size, :] = jnp.concatenate(done, axis=1).astype(bf16)
            done = []


def mix_kernel(
    gated_ref, w_ref, other_ref, single_ref, gain_ref, mixed_ref, normed_ref, held
):
    ka_count, rows, feats = gated_ref.shape
    width = single_ref.shape[1]
    chips = ka_count // 2
    at = lax.axis_index("ka")
    gated = jnp.concatenate([gated_ref[k] for k in range(ka_count)], axis=1)
    for side, ref in enumerate((w_ref, other_ref)):
        weights = ref[...].reshape(width, chips * feats)
        added = jnp.dot(gated, weights, preferred_element_type=f32)
        for flip in range(chips):
            held[at ^ (2 * flip + side)] = added[:, flip * feats : (flip + 1) * feats]
    added = jnp.concatenate([held[k] for k in range(ka_count)], axis=1)
    mixed = (single_ref[...].astype(f32) + added).astype(bf16)
    mixed_ref[...] = mixed
    normed = layer_norm(mixed.astype(f32), gain_ref[...].reshape(1, -1)).astype(bf16)
    normed_ref[...] = normed


def transition_kernel(x_ref, w_ref, out_ref):
    groups, rows, width = x_ref.shape
    part = w_ref.shape[2] // 4
    x = x_ref[...].reshape(groups * rows, width)
    down, swish, up = (
        w_ref[:, :, i * part : (i + 1) * part].reshape(width, part) for i in range(3)
    )
    a = jnp.dot(x, swish, preferred_element_type=f32)
    b = jnp.dot(x, up, preferred_element_type=f32)
    hidden = ((a / (1.0 + jnp.exp(-a))) * b).astype(bf16)
    out_ref[...] = dot_last(hidden, down).astype(bf16).reshape(groups, rows, width)


def finish_kernel(mixed_ref, part_ref, out_ref):
    total = mixed_ref[...].astype(f32)
    for i in range(part_ref.shape[0]):
        total = total + part_ref[i].astype(f32)
    out_ref[...] = total.astype(bf16)


def call(kernel, out_shape, scratch=(), scalars=0, flops=0, moved=0, limit=VMEM_LIMIT, left=()):
    def run(*operands):
        return pl.pallas_call(
            kernel,
            out_shape=out_shape,
            in_specs=[
                pl.BlockSpec(
                    memory_space=pltpu.SMEM if i < scalars else pl.ANY if i in left else pltpu.VMEM
                )
                for i in range(len(operands))
            ],
            scratch_shapes=list(scratch),
            compiler_params=pltpu.CompilerParams(vmem_limit_bytes=limit),
            cost_estimate=pl.CostEstimate(flops=flops, bytes_accessed=moved, transcendentals=0),
        )(*operands)

    return run


def on_device(
    lengths,
    single,
    attn_gain,
    w_query,
    w_key,
    w_value,
    w_gate,
    w_out,
    pair_rep,
    pair_gain,
    pair_proj,
    trans_gain,
    w_swish,
    w_up,
    w_down,
):
    grp_count = lax.axis_size("grp")
    pb_count = lax.axis_size("pb")
    ka_count = lax.axis_size("ka")
    ka_index = lax.axis_index("ka")
    samples, row_count, width = single.shape[1:]
    w_rows = w_query.shape[0]
    feats = width // ka_count
    hid = w_swish.shape[1]
    own_rows = samples * row_count
    chips = ka_count // 2
    held = ka_count // TP
    own = single.reshape(own_rows, width)

    line = [[i * 2 + c for i in range(pb_count * chips)] for c in range(2)]
    x = lax.all_gather(own, ("pb", "ka"), axis=0, tiled=False, axis_index_groups=line)

    early = [
        lax.dynamic_slice_in_dim(w, ka_index * feats, feats, 1)
        for w in (w_key, w_value, w_query, w_gate)
    ]
    early = jnp.concatenate(early + [w_down.T, w_swish, w_up, w_out], axis=1)
    early, pair_rep = lax.optimization_barrier((early, pair_rep))
    early = spread(early, pb_count, "pb")

    _, queries, key_blocks, key_rows, channels = pair_rep.shape
    keys_held = key_blocks * key_rows
    lanes = 2 * queries
    proj = pair_proj.reshape(channels, HEADS // 2, 2).transpose(2, 1, 0).reshape(HEADS, channels)
    half = jax.ShapeDtypeStruct((ka_count // 2, keys_held, lanes), f32)
    keep, one = call(
        bias_kernel,
        (half, half),
        scratch=[
            pltpu.VMEM((queries * keys_held, channels), f32),
            pltpu.VMEM((ka_count, keys_held, lanes), f32),
        ],
        flops=2 * 6 * queries * keys_held * channels * HEADS,
        moved=queries * keys_held * channels * 2 + 4 * ka_count * keys_held * lanes,
    )(pair_rep.reshape(queries, keys_held, channels), pair_gain, proj)
    one = swap(one, "ka", 1)
    two = swap(call(second_kernel, half)(keep, one), "ka", 2)
    early, two = lax.optimization_barrier((early, two))
    early = early.reshape(pb_count * w_rows, early.shape[2])

    late = early[:, 4 * feats :]
    out_w = early[:, 4 * feats + 3 * hid :]
    late = [late, swap(late, "ka", TP)]
    out_w = [late[0][:, 3 * hid :], swap(out_w, "ka", 2), late[1][:, 3 * hid :], swap(out_w, "ka", 6)]
    late = jnp.concatenate(
        [w[:, i * hid : (i + 1) * hid] for i in range(3) for w in late] + out_w, axis=1
    )
    late = jnp.broadcast_to(late[None], (grp_count,) + late.shape)
    four = swap(call(third_kernel, half)(keep, one, two), "ka", 4)
    bias = call(
        place_kernel, jax.ShapeDtypeStruct((ka_count, keys_held, lanes), f32)
    )(keep, one, two, four)

    late, attn_w, bias = lax.optimization_barrier((late, early[:, : 4 * feats], bias))
    late = exchange(late, "grp")
    attn_w = gather(attn_w, "grp")
    x, attn_w = lax.optimization_barrier((x, attn_w))
    other = swap(x, "ka", 1)

    line_rows = pb_count * chips * row_count
    kv_shape = (samples, line_rows, 2 * feats)
    query_shape = (chips * own_rows, 2 * feats)
    costs = dict(
        flops=2 * x.size * 3 * feats, moved=x.size * 2 + attn_w.size * 2, limit=MOST_VMEM
    )
    near_kv, near_query = call(
        project_kernel,
        (jax.ShapeDtypeStruct(kv_shape, bf16), jax.ShapeDtypeStruct(query_shape, f32)),
        scratch=[pltpu.VMEM(x.shape, bf16)],
        **costs,
    )(x, attn_gain, attn_w)
    gated = call(
        attention_kernel,
        jax.ShapeDtypeStruct((ka_count, own_rows, feats), bf16),
        scratch=[
            pltpu.VMEM(x.shape, bf16),
            pltpu.VMEM(kv_shape, bf16),
            pltpu.VMEM((ka_count, own_rows, feats), f32),
            pltpu.VMEM((ka_count, own_rows, feats), f32),
        ],
        scalars=1,
        **costs,
    )(lengths, other, attn_gain, attn_w, near_kv, near_query, bias)
    gated, late = lax.optimization_barrier((gated, late))
    gated = exchange(gated, "ka")
    out_w = late[:, :, held * 3 * hid :]
    other_w = swap(out_w, "ka", 1)

    rows = jax.ShapeDtypeStruct((own_rows, width), bf16)
    shared = jax.ShapeDtypeStruct((TP, own_rows, width), bf16)
    mixed, normed_t = call(
        mix_kernel,
        (rows, rows),
        scratch=[pltpu.VMEM((ka_count, own_rows, feats), f32)],
        flops=2 * own_rows * width * width,
        moved=width * width * 2,
    )(gated, out_w, other_w, own, trans_gain)

    groups = [list(range(i, i + TP)) for i in range(0, ka_count, TP)]
    normed_t = lax.all_gather(normed_t, "ka", axis=0, tiled=False, axis_index_groups=groups)
    part = call(
        transition_kernel,
        shared,

        flops=2 * own_rows * width * hid * ka_count * 3,
        moved=3 * width * hid * ka_count // TP * 2,
    )(normed_t, late)
    part = exchange(part, "ka", groups)
    result = call(finish_kernel, rows)(mixed, part)
    return result.reshape(1, samples, row_count, width)


def solution(mesh):
    return jax.shard_map(
        on_device,
        mesh=mesh,
        in_specs=(
            P("grp"),
            P("grp", None, ("pb", "ka"), None),
            P(),
            P(("grp", "pb"), None),
            P(("grp", "pb"), None),
            P(("grp", "pb"), None),
            P(("grp", "pb"), None),
            P(("grp", "pb"), "ka"),
            P("grp", "pb", None, "ka", None),
            P(),
            P(),
            P(),
            P(("grp", "pb"), "ka"),
            P(("grp", "pb"), "ka"),
            P("ka", ("grp", "pb")),
        ),
        out_specs=P("grp", None, ("pb", "ka"), None),
        check_vma=False,
    )
```

```python
import functools
import math

import jax
import jax.numpy as jnp
from jax import lax
from jax.experimental import pallas as pl
from jax.experimental.pallas import tpu as pltpu
from jax.sharding import PartitionSpec as P

HEADS = 16
TP = 4

epsilon = 1e-05
very_negative = -1e30
f32 = jnp.float32
bf16 = jnp.bfloat16
VMEM_LIMIT = 32 * 1024 * 1024
MOST_VMEM = 32 * 1024 * 1024


def layer_norm(inputs, scale_gain):
    mean_val = jnp.mean(inputs, axis=-1, keepdims=True)
    centred = inputs - mean_val
    spread = jnp.mean(centred * centred, axis=-1, keepdims=True)
    return centred * lax.rsqrt(spread + epsilon) * scale_gain


def dot_last(a, b, precision=None):
    return lax.dot_general(
        a, b, (((1,), (1,)), ((), ())), preferred_element_type=f32, precision=precision
    )


def exchange(blocks, axes, groups=None):
    return lax.all_to_all(
        blocks, axes, split_axis=0, concat_axis=0, tiled=True, axis_index_groups=groups
    )


def spread(block, count, axes):
    return exchange(jnp.broadcast_to(block[None], (count,) + block.shape), axes)


def gather(block, axes):
    return lax.all_gather(block, axes, axis=0, tiled=False)


def swap(block, axis, flip):
    count = lax.axis_size(axis)
    return lax.ppermute(block, axis, [(i, i ^ flip) for i in range(count)])


def bias_kernel(x_ref, gain_ref, proj_ref, *refs):
    out_refs, rows, held = refs[:-2], refs[-2], refs[-1]
    queries, keys, channels = x_ref.shape
    pairs = len(out_refs)
    normed = layer_norm(
        x_ref[...].reshape(queries * keys, channels).astype(f32), gain_ref[...].reshape(1, -1)
    )
    rows[...] = normed
    together = 256 // queries
    for start in range(0, keys, together):
        block = jnp.concatenate(
            [rows[pl.ds(start + j, queries, stride=keys), :] for j in range(together)], axis=0
        )
        bias = dot_last(proj_ref[...], block, lax.Precision.HIGHEST)
        for j in range(together):
            cols = slice(j * queries, (j + 1) * queries)
            tile = jnp.concatenate([bias[:pairs, cols], bias[pairs:, cols]], axis=1)
            held[:, start + j, :] = tile
    for flip, out_ref in enumerate(out_refs):
        out_ref[...] = held[lax.axis_index("ka") ^ flip]


def place_kernel(*refs):
    for flip, ref in enumerate(refs[:-1]):
        refs[-1][lax.axis_index("ka") ^ flip] = ref[...]


def project_side(samples, x_ref, gain_ref, w_ref, held_ref, kv_ref):
    places, own_rows, width = x_ref.shape
    feats = kv_ref.shape[2] // 2
    each = own_rows // samples
    chips = places // lax.axis_size("pb")
    weights = w_ref[...].reshape(width, 4 * feats)
    x = x_ref[...].reshape(places * own_rows, width).astype(f32)
    normed = layer_norm(x, gain_ref[...].reshape(1, -1)).astype(bf16)
    held_ref[...] = normed.reshape(places, own_rows, width)
    proj = jnp.dot(normed, weights[:, : 2 * feats], preferred_element_type=f32)
    proj = proj.reshape(places, samples, each, 2 * feats)
    for s in range(samples):
        kv_ref[s] = proj[:, s].reshape(places * each, 2 * feats).astype(bf16)
    rows = held_ref[pl.ds(lax.axis_index("pb") * chips, chips)].reshape(chips * own_rows, width)
    return jnp.dot(rows, weights[:, 2 * feats :], preferred_element_type=f32)


def project_kernel(x_ref, gain_ref, w_ref, kv_ref, query_ref, held_ref):
    samples = kv_ref.shape[0]
    query_ref[...] = project_side(samples, x_ref, gain_ref, w_ref, held_ref, kv_ref)


def attention_kernel(length_ref, x_ref, gain_ref, w_ref, kv_ref, near_ref, bias_ref, *refs):
    out_ref, held_normed, held_kv, held_query, held_gate = refs
    count, keys_held, lanes = bias_ref.shape
    places, own_rows, width = x_ref.shape
    samples, span, feats = kv_ref.shape
    feats = feats // 2
    chips = count // 2
    blocks = places // chips
    q_rows = lanes // 2
    each = q_rows // count
    key_count = blocks * q_rows
    head_dim = feats // 2
    length, at = length_ref[0], lax.axis_index("ka")
    core = at % 2
    far = project_side(samples, x_ref, gain_ref, w_ref, held_normed, held_kv)
    for side, proj in enumerate((near_ref[...], far)):
        for z in range(chips):
            k = 2 * z + (core ^ side)
            part = proj[z * own_rows : (z + 1) * own_rows]
            held_query[k] = part[:, :feats]
            held_gate[k] = part[:, feats:]
    bias = jnp.concatenate(
        [
            bias_ref[2 * z + (core ^ side), b * each : (b + 1) * each, :]
            for side in range(2)
            for b in range(blocks)
            for z in range(chips)
        ],
        axis=0,
    )
    index = lax.broadcasted_iota(jnp.int32, (key_count, lanes), 0)
    side = index // span
    position = ((index % span) // each) * (2 * each) + (side ^ core) * each + index % each
    live = position < length
    first = lax.broadcasted_iota(jnp.int32, (q_rows, feats), 1) < head_dim
    done = []
    for s in range(samples):
        both_sides = jnp.concatenate([kv_ref[s], held_kv[s]], axis=0)
        keys, values = both_sides[:, :feats], both_sides[:, feats:]
        rows = slice(s * each, (s + 1) * each)
        query = held_query[:, rows, :].reshape(q_rows, feats)
        both = jnp.concatenate(
            [jnp.where(first, query, 0.0), jnp.where(first, 0.0, query)], axis=0
        ).astype(bf16)
        scores = dot_last(keys, both) * (1.0 / math.sqrt(head_dim)) + bias
        scores = jnp.where(live, scores, very_negative)
        peak = jnp.max(scores, axis=0, keepdims=True)
        soft = jnp.exp(scores - peak)
        total = jnp.sum(soft, axis=0, keepdims=True)
        weighted = lax.dot_general(
            values, soft.astype(bf16), (((0,), (0,)), ((), ())), preferred_element_type=f32
        )
        attended = (weighted / total).T
        attended = jnp.where(first, attended[:q_rows], attended[q_rows:])
        gate = jax.nn.sigmoid(held_gate[:, rows, :].reshape(q_rows, feats))
        gate = gate.astype(bf16).astype(f32)
        done.append((attended * gate).reshape(count, each, feats))
        if s % 2:
            size = 2 * each
            start = s // 2 * size
            out_ref[:, start : start + size, :] = jnp.concatenate(done, axis=1).astype(bf16)
            done = []


def mix_kernel(
    gated_ref, w_ref, other_ref, single_ref, gain_ref, mixed_ref, normed_ref, held
):
    ka_count, rows, feats = gated_ref.shape
    width = single_ref.shape[1]
    chips = ka_count // 2
    at = lax.axis_index("ka")
    gated = jnp.concatenate([gated_ref[k] for k in range(ka_count)], axis=1)
    for side, ref in enumerate((w_ref, other_ref)):
        weights = ref[...].reshape(width, chips * feats)
        added = jnp.dot(gated, weights, preferred_element_type=f32)
        for flip in range(chips):
            held[at ^ (2 * flip + side)] = added[:, flip * feats : (flip + 1) * feats]
    added = jnp.concatenate([held[k] for k in range(ka_count)], axis=1)
    mixed = (single_ref[...].astype(f32) + added).astype(bf16)
    mixed_ref[...] = mixed
    normed = layer_norm(mixed.astype(f32), gain_ref[...].reshape(1, -1)).astype(bf16)
    normed_ref[...] = normed


def transition_kernel(x_ref, w_ref, out_ref):
    groups, rows, width = x_ref.shape
    part = w_ref.shape[2] // 4
    x = x_ref[...].reshape(groups * rows, width)
    down, swish, up = (
        w_ref[:, :, i * part : (i + 1) * part].reshape(width, part) for i in range(3)
    )
    a = jnp.dot(x, swish, preferred_element_type=f32)
    b = jnp.dot(x, up, preferred_element_type=f32)
    hidden = ((a / (1.0 + jnp.exp(-a))) * b).astype(bf16)
    out_ref[...] = dot_last(hidden, down).astype(bf16).reshape(groups, rows, width)


def finish_kernel(mixed_ref, part_ref, out_ref):
    total = mixed_ref[...].astype(f32)
    for i in range(part_ref.shape[0]):
        total = total + part_ref[i].astype(f32)
    out_ref[...] = total.astype(bf16)


def call(kernel, out_shape, scratch=(), scalars=0, flops=0, moved=0, limit=VMEM_LIMIT, left=()):
    def run(*operands):
        return pl.pallas_call(
            kernel,
            out_shape=out_shape,
            in_specs=[
                pl.BlockSpec(
                    memory_space=pltpu.SMEM if i < scalars else pl.ANY if i in left else pltpu.VMEM
                )
                for i in range(len(operands))
            ],
            scratch_shapes=list(scratch),
            compiler_params=pltpu.CompilerParams(vmem_limit_bytes=limit),
            cost_estimate=pl.CostEstimate(flops=flops, bytes_accessed=moved, transcendentals=0),
        )(*operands)

    return run


def on_device(
    lengths,
    single,
    attn_gain,
    w_query,
    w_key,
    w_value,
    w_gate,
    w_out,
    pair_rep,
    pair_gain,
    pair_proj,
    trans_gain,
    w_swish,
    w_up,
    w_down,
):
    grp_count = lax.axis_size("grp")
    pb_count = lax.axis_size("pb")
    ka_count = lax.axis_size("ka")
    ka_index = lax.axis_index("ka")
    samples, row_count, width = single.shape[1:]
    w_rows = w_query.shape[0]
    feats = width // ka_count
    hid = w_swish.shape[1]
    own_rows = samples * row_count
    chips = ka_count // 2
    held = ka_count // TP
    own = single.reshape(own_rows, width)

    line = [[i * 2 + c for i in range(pb_count * chips)] for c in range(2)]
    x = lax.all_gather(own, ("pb", "ka"), axis=0, tiled=False, axis_index_groups=line)

    early = [
        lax.dynamic_slice_in_dim(w, ka_index * feats, feats, 1)
        for w in (w_key, w_value, w_query, w_gate)
    ]
    early = jnp.concatenate(early + [w_down.T, w_swish, w_up, w_out], axis=1)
    early, pair_rep = lax.optimization_barrier((early, pair_rep))
    early = spread(early, pb_count, "pb")

    _, queries, key_blocks, key_rows, channels = pair_rep.shape
    keys_held = key_blocks * key_rows
    lanes = 2 * queries
    proj = pair_proj.reshape(channels, HEADS // 2, 2).transpose(2, 1, 0).reshape(HEADS, channels)
    bias = call(
        bias_kernel,
        (jax.ShapeDtypeStruct((keys_held, lanes), f32),) * ka_count,
        scratch=[
            pltpu.VMEM((queries * keys_held, channels), f32),
            pltpu.VMEM((ka_count, keys_held, lanes), f32),
        ],
        flops=2 * 6 * queries * keys_held * channels * HEADS,
        moved=queries * keys_held * channels * 2 + 4 * ka_count * keys_held * lanes,
    )(pair_rep.reshape(queries, keys_held, channels), pair_gain, proj)
    near = [swap(bias[i], "ka", i) for i in (1, 2, 3)]
    early, near = lax.optimization_barrier((early, near))
    early = early.reshape(pb_count * w_rows, early.shape[2])

    attn_w = jnp.broadcast_to(early[None, :, : 4 * feats], (grp_count, pb_count * w_rows, 4 * feats))
    late = early[:, 4 * feats :]
    out_w = early[:, 4 * feats + 3 * hid :]
    attn_w, late, out_w = lax.optimization_barrier((attn_w, late, out_w))
    attn_w = exchange(attn_w, "grp")

    farthest = swap(out_w, "ka", 6)
    half = swap(late, "ka", TP)
    out_w, half = lax.optimization_barrier((out_w, half))
    late = [late, half]
    out_w = [late[0][:, 3 * hid :], swap(out_w, "ka", 2), late[1][:, 3 * hid :], farthest]
    late = jnp.concatenate(
        [w[:, i * hid : (i + 1) * hid] for i in range(3) for w in late] + out_w, axis=1
    )
    late = jnp.broadcast_to(late[None], (grp_count,) + late.shape)
    late, attn_w, far = lax.optimization_barrier((late, attn_w, list(bias[4:])))
    late = exchange(late, "grp")
    far = [swap(block, "ka", i + 4) for i, block in enumerate(far)]
    bias = call(
        place_kernel, jax.ShapeDtypeStruct((ka_count, keys_held, lanes), f32)
    )(bias[0], *near, *far)
    x, bias = lax.optimization_barrier((x, bias))
    other = swap(x, "ka", 1)

    line_rows = pb_count * chips * row_count
    kv_shape = (samples, line_rows, 2 * feats)
    query_shape = (chips * own_rows, 2 * feats)
    costs = dict(
        flops=2 * x.size * 3 * feats, moved=x.size * 2 + attn_w.size * 2, limit=MOST_VMEM
    )
    near_kv, near_query = call(
        project_kernel,
        (jax.ShapeDtypeStruct(kv_shape, bf16), jax.ShapeDtypeStruct(query_shape, f32)),
        scratch=[pltpu.VMEM(x.shape, bf16)],
        **costs,
    )(x, attn_gain, attn_w)
    gated = call(
        attention_kernel,
        jax.ShapeDtypeStruct((ka_count, own_rows, feats), bf16),
        scratch=[
            pltpu.VMEM(x.shape, bf16),
            pltpu.VMEM(kv_shape, bf16),
            pltpu.VMEM((ka_count, own_rows, feats), f32),
            pltpu.VMEM((ka_count, own_rows, feats), f32),
        ],
        scalars=1,
        **costs,
    )(lengths, other, attn_gain, attn_w, near_kv, near_query, bias)
    gated, late = lax.optimization_barrier((gated, late))
    gated = exchange(gated, "ka")
    out_w = late[:, :, held * 3 * hid :]
    other_w = swap(out_w, "ka", 1)

    rows = jax.ShapeDtypeStruct((own_rows, width), bf16)
    shared = jax.ShapeDtypeStruct((TP, own_rows, width), bf16)
    mixed, normed_t = call(
        mix_kernel,
        (rows, rows),
        scratch=[pltpu.VMEM((ka_count, own_rows, feats), f32)],
        flops=2 * own_rows * width * width,
        moved=width * width * 2,
    )(gated, out_w, other_w, own, trans_gain)

    groups = [list(range(i, i + TP)) for i in range(0, ka_count, TP)]
    normed_t = lax.all_gather(normed_t, "ka", axis=0, tiled=False, axis_index_groups=groups)
    part = call(
        transition_kernel,
        shared,

        flops=2 * own_rows * width * hid * ka_count * 3,
        moved=3 * width * hid * ka_count // TP * 2,
    )(normed_t, late)
    part = exchange(part, "ka", groups)
    result = call(finish_kernel, rows)(mixed, part)
    return result.reshape(1, samples, row_count, width)


def solution(mesh):
    return jax.shard_map(
        on_device,
        mesh=mesh,
        in_specs=(
            P("grp"),
            P("grp", None, ("pb", "ka"), None),
            P(),
            P(("grp", "pb"), None),
            P(("grp", "pb"), None),
            P(("grp", "pb"), None),
            P(("grp", "pb"), None),
            P(("grp", "pb"), "ka"),
            P("grp", "pb", None, "ka", None),
            P(),
            P(),
            P(),
            P(("grp", "pb"), "ka"),
            P(("grp", "pb"), "ka"),
            P("ka", ("grp", "pb")),
        ),
        out_specs=P("grp", None, ("pb", "ka"), None),
        check_vma=False,
    )
```

```python
import functools
import math

import jax
import jax.numpy as jnp
from jax import lax
from jax.experimental import pallas as pl
from jax.experimental.pallas import tpu as pltpu
from jax.sharding import PartitionSpec as P

HEADS = 16
TP = 4

epsilon = 1e-05
very_negative = -1e30
f32 = jnp.float32
bf16 = jnp.bfloat16
VMEM_LIMIT = 32 * 1024 * 1024
MOST_VMEM = 32 * 1024 * 1024


def layer_norm(inputs, scale_gain):
    mean_val = jnp.mean(inputs, axis=-1, keepdims=True)
    centred = inputs - mean_val
    spread = jnp.mean(centred * centred, axis=-1, keepdims=True)
    return centred * lax.rsqrt(spread + epsilon) * scale_gain


def dot_last(a, b, precision=None):
    return lax.dot_general(
        a, b, (((1,), (1,)), ((), ())), preferred_element_type=f32, precision=precision
    )


def exchange(blocks, axes, groups=None):
    return lax.all_to_all(
        blocks, axes, split_axis=0, concat_axis=0, tiled=True, axis_index_groups=groups
    )


def spread(block, count, axes):
    return exchange(jnp.broadcast_to(block[None], (count,) + block.shape), axes)


def gather(block, axes):
    return lax.all_gather(block, axes, axis=0, tiled=False)


def swap(block, axis, flip):
    count = lax.axis_size(axis)
    return lax.ppermute(block, axis, [(i, i ^ flip) for i in range(count)])


def bias_kernel(x_ref, gain_ref, proj_ref, keep_ref, send_ref, rows, held):
    queries, keys, channels = x_ref.shape
    pairs = held.shape[0]
    normed = layer_norm(
        x_ref[...].reshape(queries * keys, channels).astype(f32), gain_ref[...].reshape(1, -1)
    )
    rows[...] = normed
    together = 256 // queries
    for start in range(0, keys, together):
        block = jnp.concatenate(
            [rows[pl.ds(start + j, queries, stride=keys), :] for j in range(together)], axis=0
        )
        bias = dot_last(proj_ref[...], block, lax.Precision.HIGHEST)
        for j in range(together):
            cols = slice(j * queries, (j + 1) * queries)
            tile = jnp.concatenate([bias[:pairs, cols], bias[pairs:, cols]], axis=1)
            held[:, start + j, :] = tile
    for i in range(pairs // 2):
        keep_ref[i] = held[lax.axis_index("ka") ^ (2 * i)]
        send_ref[i] = held[lax.axis_index("ka") ^ (2 * i + 1)]


def second_kernel(keep_ref, one_ref, out_ref):
    for i in range(2):
        out_ref[2 * i] = keep_ref[2 * i + 1]
        out_ref[2 * i + 1] = one_ref[2 * i + 1]


def third_kernel(keep_ref, one_ref, two_ref, out_ref):
    out_ref[0] = keep_ref[2]
    out_ref[1] = one_ref[2]
    out_ref[2] = two_ref[2]
    out_ref[3] = two_ref[3]


def place_kernel(keep_ref, one_ref, two_ref, four_ref, out_ref):
    at = lax.axis_index("ka")
    out_ref[at] = keep_ref[0]
    out_ref[at ^ 1] = one_ref[0]
    out_ref[at ^ 2] = two_ref[0]
    out_ref[at ^ 3] = two_ref[1]
    for i in range(four_ref.shape[0]):
        out_ref[at ^ (4 + i)] = four_ref[i]


def project_side(samples, x_ref, gain_ref, w_ref, held_ref, kv_ref):
    places, own_rows, width = x_ref.shape
    feats = kv_ref.shape[2] // 2
    each = own_rows // samples
    chips = places // lax.axis_size("pb")
    weights = w_ref[:, :, : 4 * feats].reshape(width, 4 * feats)
    x = x_ref[...].reshape(places * own_rows, width).astype(f32)
    normed = layer_norm(x, gain_ref[...].reshape(1, -1)).astype(bf16)
    held_ref[...] = normed.reshape(places, own_rows, width)
    proj = jnp.dot(normed, weights[:, : 2 * feats], preferred_element_type=f32)
    proj = proj.reshape(places, samples, each, 2 * feats)
    for s in range(samples):
        kv_ref[s] = proj[:, s].reshape(places * each, 2 * feats).astype(bf16)
    rows = held_ref[pl.ds(lax.axis_index("pb") * chips, chips)].reshape(chips * own_rows, width)
    return jnp.dot(rows, weights[:, 2 * feats :], preferred_element_type=f32)


def project_kernel(x_ref, gain_ref, w_ref, kv_ref, query_ref, held_ref):
    samples = kv_ref.shape[0]
    query_ref[...] = project_side(samples, x_ref, gain_ref, w_ref, held_ref, kv_ref)


def attention_kernel(length_ref, x_ref, gain_ref, w_ref, kv_ref, near_ref, bias_ref, *refs):
    out_ref, held_normed, held_kv, held_query, held_gate = refs
    count, keys_held, lanes = bias_ref.shape
    places, own_rows, width = x_ref.shape
    samples, span, feats = kv_ref.shape
    feats = feats // 2
    chips = count // 2
    blocks = places // chips
    q_rows = lanes // 2
    each = q_rows // count
    key_count = blocks * q_rows
    head_dim = feats // 2
    length, at = length_ref[0], lax.axis_index("ka")
    core = at % 2
    far = project_side(samples, x_ref, gain_ref, w_ref, held_normed, held_kv)
    for side, proj in enumerate((near_ref[...], far)):
        for z in range(chips):
            k = 2 * z + (core ^ side)
            part = proj[z * own_rows : (z + 1) * own_rows]
            held_query[k] = part[:, :feats]
            held_gate[k] = part[:, feats:]
    bias = jnp.concatenate(
        [
            bias_ref[2 * z + (core ^ side), b * each : (b + 1) * each, :]
            for side in range(2)
            for b in range(blocks)
            for z in range(chips)
        ],
        axis=0,
    )
    index = lax.broadcasted_iota(jnp.int32, (key_count, lanes), 0)
    side = index // span
    position = ((index % span) // each) * (2 * each) + (side ^ core) * each + index % each
    live = position < length
    first = lax.broadcasted_iota(jnp.int32, (q_rows, feats), 1) < head_dim
    done = []
    for s in range(samples):
        both_sides = jnp.concatenate([kv_ref[s], held_kv[s]], axis=0)
        keys, values = both_sides[:, :feats], both_sides[:, feats:]
        rows = slice(s * each, (s + 1) * each)
        query = held_query[:, rows, :].reshape(q_rows, feats)
        both = jnp.concatenate(
            [jnp.where(first, query, 0.0), jnp.where(first, 0.0, query)], axis=0
        ).astype(bf16)
        scores = dot_last(keys, both) * (1.0 / math.sqrt(head_dim)) + bias
        scores = jnp.where(live, scores, very_negative)
        peak = jnp.max(scores, axis=0, keepdims=True)
        soft = jnp.exp(scores - peak)
        total = jnp.sum(soft, axis=0, keepdims=True)
        weighted = lax.dot_general(
            values, soft.astype(bf16), (((0,), (0,)), ((), ())), preferred_element_type=f32
        )
        attended = (weighted / total).T
        attended = jnp.where(first, attended[:q_rows], attended[q_rows:])
        gate = jax.nn.sigmoid(held_gate[:, rows, :].reshape(q_rows, feats))
        gate = gate.astype(bf16).astype(f32)
        done.append((attended * gate).reshape(count, each, feats))
        if s % 2:
            size = 2 * each
            start = s // 2 * size
            out_ref[:, start : start + size, :] = jnp.concatenate(done, axis=1).astype(bf16)
            done = []


def mix_kernel(
    gated_ref, w_ref, other_ref, single_ref, gain_ref, mixed_ref, normed_ref, held
):
    ka_count, rows, feats = gated_ref.shape
    width = single_ref.shape[1]
    chips = ka_count // 2
    at = lax.axis_index("ka")
    gated = jnp.concatenate([gated_ref[k] for k in range(ka_count)], axis=1)
    for side, ref in enumerate((w_ref, other_ref)):
        weights = ref[...].reshape(width, chips * feats)
        added = jnp.dot(gated, weights, preferred_element_type=f32)
        for i, flip in enumerate((0, 4, 2, 6)):
            held[at ^ (flip + side)] = added[:, i * feats : (i + 1) * feats]
    added = jnp.concatenate([held[k] for k in range(ka_count)], axis=1)
    mixed = (single_ref[...].astype(f32) + added).astype(bf16)
    mixed_ref[...] = mixed
    normed = layer_norm(mixed.astype(f32), gain_ref[...].reshape(1, -1)).astype(bf16)
    normed_ref[...] = normed


def transition_kernel(x_ref, w_ref, out_ref):
    groups, rows, width = x_ref.shape
    part = w_ref.shape[2] // 3
    x = x_ref[...].reshape(groups * rows, width)
    down, swish, up = (
        w_ref[:, :, i * part : (i + 1) * part].reshape(width, part) for i in range(3)
    )
    a = jnp.dot(x, swish, preferred_element_type=f32)
    b = jnp.dot(x, up, preferred_element_type=f32)
    hidden = ((a / (1.0 + jnp.exp(-a))) * b).astype(bf16)
    out_ref[...] = dot_last(hidden, down).astype(bf16).reshape(groups, rows, width)


def finish_kernel(mixed_ref, part_ref, out_ref):
    total = mixed_ref[...].astype(f32)
    for i in range(part_ref.shape[0]):
        total = total + part_ref[i].astype(f32)
    out_ref[...] = total.astype(bf16)


def call(kernel, out_shape, scratch=(), scalars=0, flops=0, moved=0, limit=VMEM_LIMIT, left=()):
    def run(*operands):
        return pl.pallas_call(
            kernel,
            out_shape=out_shape,
            in_specs=[
                pl.BlockSpec(
                    memory_space=pltpu.SMEM if i < scalars else pl.ANY if i in left else pltpu.VMEM
                )
                for i in range(len(operands))
            ],
            scratch_shapes=list(scratch),
            compiler_params=pltpu.CompilerParams(vmem_limit_bytes=limit),
            cost_estimate=pl.CostEstimate(flops=flops, bytes_accessed=moved, transcendentals=0),
        )(*operands)

    return run


def on_device(
    lengths,
    single,
    attn_gain,
    w_query,
    w_key,
    w_value,
    w_gate,
    w_out,
    pair_rep,
    pair_gain,
    pair_proj,
    trans_gain,
    w_swish,
    w_up,
    w_down,
):
    grp_count = lax.axis_size("grp")
    pb_count = lax.axis_size("pb")
    ka_count = lax.axis_size("ka")
    ka_index = lax.axis_index("ka")
    samples, row_count, width = single.shape[1:]
    w_rows = w_query.shape[0]
    feats = width // ka_count
    hid = w_swish.shape[1]
    own_rows = samples * row_count
    chips = ka_count // 2
    held = ka_count // TP
    own = single.reshape(own_rows, width)

    line = [[i * 2 + c for i in range(pb_count * chips)] for c in range(2)]
    x = lax.all_gather(own, ("pb", "ka"), axis=0, tiled=False, axis_index_groups=line)

    early = [
        lax.dynamic_slice_in_dim(w, ka_index * feats, feats, 1)
        for w in (w_key, w_value, w_query, w_gate)
    ]
    early = jnp.concatenate(early + [w_out, w_down.T, w_swish, w_up], axis=1)
    early, pair_rep = lax.optimization_barrier((early, pair_rep))
    early = spread(early, pb_count, "pb")

    _, queries, key_blocks, key_rows, channels = pair_rep.shape
    keys_held = key_blocks * key_rows
    lanes = 2 * queries
    proj = pair_proj.reshape(channels, HEADS // 2, 2).transpose(2, 1, 0).reshape(HEADS, channels)
    half = jax.ShapeDtypeStruct((ka_count // 2, keys_held, lanes), f32)
    keep, one = call(
        bias_kernel,
        (half, half),
        scratch=[
            pltpu.VMEM((queries * keys_held, channels), f32),
            pltpu.VMEM((ka_count, keys_held, lanes), f32),
        ],
        flops=2 * 6 * queries * keys_held * channels * HEADS,
        moved=queries * keys_held * channels * 2 + 4 * ka_count * keys_held * lanes,
    )(pair_rep.reshape(queries, keys_held, channels), pair_gain, proj)
    one = swap(one, "ka", 1)
    two = swap(call(second_kernel, half)(keep, one), "ka", 2)
    early, two = lax.optimization_barrier((early, two))
    early = early.reshape(pb_count * w_rows, early.shape[2])

    split = 5 * feats
    attn_w = jnp.broadcast_to(early[None, :, :split], (grp_count, pb_count * w_rows, split))
    late = early[:, split:]
    attn_w = exchange(attn_w, "grp")

    late = [late, swap(late, "ka", TP)]
    late = jnp.concatenate([w[:, i * hid : (i + 1) * hid] for i in range(3) for w in late], axis=1)
    late = jnp.broadcast_to(late[None], (grp_count,) + late.shape)
    four = swap(call(third_kernel, half)(keep, one, two), "ka", 4)
    bias = call(
        place_kernel, jax.ShapeDtypeStruct((ka_count, keys_held, lanes), f32)
    )(keep, one, two, four)
    late, attn_w, bias = lax.optimization_barrier((late, attn_w, bias))
    late = exchange(late, "grp")

    out_w = attn_w[:, :, 4 * feats :]
    for flip in (4, 2):
        out_w = jnp.concatenate([out_w, swap(out_w, "ka", flip)], axis=2)
    x, late, out_w = lax.optimization_barrier((x, late, out_w))
    other = swap(x, "ka", 1)
    other_w = swap(out_w, "ka", 1)

    line_rows = pb_count * chips * row_count
    kv_shape = (samples, line_rows, 2 * feats)
    query_shape = (chips * own_rows, 2 * feats)
    costs = dict(
        flops=2 * x.size * 3 * feats, moved=x.size * 2 + attn_w.size * 2, limit=MOST_VMEM
    )
    near_kv, near_query = call(
        project_kernel,
        (jax.ShapeDtypeStruct(kv_shape, bf16), jax.ShapeDtypeStruct(query_shape, f32)),
        scratch=[pltpu.VMEM(x.shape, bf16)],
        **costs,
    )(x, attn_gain, attn_w)
    gated = call(
        attention_kernel,
        jax.ShapeDtypeStruct((ka_count, own_rows, feats), bf16),
        scratch=[
            pltpu.VMEM(x.shape, bf16),
            pltpu.VMEM(kv_shape, bf16),
            pltpu.VMEM((ka_count, own_rows, feats), f32),
            pltpu.VMEM((ka_count, own_rows, feats), f32),
        ],
        scalars=1,
        **costs,
    )(lengths, other, attn_gain, attn_w, near_kv, near_query, bias)
    gated = exchange(gated, "ka")

    rows = jax.ShapeDtypeStruct((own_rows, width), bf16)
    shared = jax.ShapeDtypeStruct((TP, own_rows, width), bf16)
    mixed, normed_t = call(
        mix_kernel,
        (rows, rows),
        scratch=[pltpu.VMEM((ka_count, own_rows, feats), f32)],
        flops=2 * own_rows * width * width,
        moved=width * width * 2,
    )(gated, out_w, other_w, own, trans_gain)

    groups = [list(range(i, i + TP)) for i in range(0, ka_count, TP)]
    normed_t = lax.all_gather(normed_t, "ka", axis=0, tiled=False, axis_index_groups=groups)
    part = call(
        transition_kernel,
        shared,

        flops=2 * own_rows * width * hid * ka_count * 3,
        moved=3 * width * hid * ka_count // TP * 2,
    )(normed_t, late)
    part = exchange(part, "ka", groups)
    result = call(finish_kernel, rows)(mixed, part)
    return result.reshape(1, samples, row_count, width)


def solution(mesh):
    return jax.shard_map(
        on_device,
        mesh=mesh,
        in_specs=(
            P("grp"),
            P("grp", None, ("pb", "ka"), None),
            P(),
            P(("grp", "pb"), None),
            P(("grp", "pb"), None),
            P(("grp", "pb"), None),
            P(("grp", "pb"), None),
            P(("grp", "pb"), "ka"),
            P("grp", "pb", None, "ka", None),
            P(),
            P(),
            P(),
            P(("grp", "pb"), "ka"),
            P(("grp", "pb"), "ka"),
            P("ka", ("grp", "pb")),
        ),
        out_specs=P("grp", None, ("pb", "ka"), None),
        check_vma=False,
    )
```
